128 devices in a mesh: row: 8 (over x, core), col: 16 (over z, y).
Axes of the slice: x: 4, y: 4, z: 4, core: 2. Of those that a mesh axis runs over, the one named last changes fastest.
Arguments:
- a_tiles: bfloat16 [8, 768, 128, 128], P('row', 'col'), may hold values from -0.21875 to 0.21875
- a_rows: int32 [8, 768], P('row', 'col'), may hold values from 0 to 31, as said below
- a_cols: int32 [8, 768], P('row', 'col'), may hold values from 0 to 15
- p_tiles: bfloat16 [128, 16, 128, 128], P('row', 'col'), may hold values from -6 to 6
- p_pos: int32 [128, 16], P('row', 'col'), may hold values from 0 to 63, as said below
- r_tiles: bfloat16 [256, 128, 128], P('row'), may hold values from -0.5 to 0.5
- aggregate: int32 [256, 1], P('row'), may hold values from 0 to 31; in each aligned block of 32 rows (0 to 31, 32 to 63, ...) at most 2 rows name the same one
Outputs:
- product: bfloat16 [32768, 4096], P('row', 'col')
- coarse: float32 [4096, 4096], P('row', 'col')
The draws below stay inside these ranges and needn't reach their ends.
Inputs may be any that keep to these rules, and one draw needn't show every extreme that they name: `p_pos`: within one device's block the positions are distinct. `a_rows`: among the 48 tiles of one device, every fine tile row is named 48 // 32 times or once more, so at most 2 times. `aggregate`: among the 32 fine tile rows of one index of row, no coarse tile row is named more than 2 times.
All inputs are finite; a program needn't handle non-finite values.
Results may differ from the reference program's by a relative error of at most 0.01.
Values may be sent and summed in bfloat16 or wider, within the bound.
A program may use at most 192 MiB of HBM per device.

```python
import math
import jax
import jax.numpy as jnp
import numpy as np
from jax import lax

B = 128
RT_DEV = 32
A_DEV = 48
P_DEV = 16
CT_DEV = 2
MOST = 2
NT = 256
N = 32768
KT_DEV = 16
CT = 32
NC = 4096
N_ROW = 8
N_COL = 16


def draw_p_pos(key, part):
    key = jax.random.fold_in(key, 7)
    slots = RT_DEV * CT_DEV
    scores = jax.random.randint(key, (N_ROW, N_COL, slots), 0, 1 << 20)
    scores = scores * slots + jnp.arange(slots, dtype=jnp.int32)[None, None, :]
    order = jnp.argsort(scores, axis=2)[:, :, :P_DEV].astype(jnp.int32)
    return jnp.transpose(order, (0, 2, 1)).reshape(N_ROW * P_DEV, N_COL)


def draw_a_rows(key, part):
    key = jax.random.fold_in(key, 11)
    key_shift, key_order = jax.random.split(key)
    shift = jax.random.randint(key_shift, (N_ROW, N_COL, 1), 0, RT_DEV)
    base = (jnp.arange(A_DEV, dtype=jnp.int32)[None, None, :] + shift) % RT_DEV
    scores = jax.random.randint(key_order, (N_ROW, N_COL, A_DEV), 0, 1 << 20)
    scores = scores * A_DEV + jnp.arange(A_DEV, dtype=jnp.int32)[None, None, :]
    order = jnp.argsort(scores, axis=2).astype(jnp.int32)
    mixed = jnp.take_along_axis(base, order, axis=2)
    return mixed.reshape(N_ROW, N_COL * A_DEV).astype(jnp.int32)


def plant(drawn, stream_key, least, largest):
    extent = drawn.shape
    place = [jax.random.randint(jax.random.fold_in(stream_key, axis), (), 0, extent[axis]) for axis in range(len(extent))]
    drawn = drawn.at[tuple(place)].set(least)
    longest = extent.index(max(extent))
    place[longest] = (place[longest] + 1) % extent[longest]
    return drawn.at[tuple(place)].set(largest)


def block_scale(rng, shape, cuts, least, largest):
    factor_of, own = 1.0, jax.random.fold_in(rng, 6)
    for axis_at, blocks in cuts:
        draws = jnp.exp(jax.random.uniform(jax.random.fold_in(own, axis_at), (blocks,), jnp.float32, least / len(cuts), largest / len(cuts)))
        factor_of = factor_of * jnp.repeat(draws, shape[axis_at] // blocks).reshape([-1 if axis == axis_at else 1 for axis in range(len(shape))])
    return factor_of


def deal_out(rng, own, number, rows, amount, top, limit, skew):
    ranking = jax.random.permutation(rng, amount)
    packed, usual = portions_of(amount, rows * top, limit, skew, True), portions_of(amount, rows * top, limit, skew, False)
    places = jnp.arange(amount)

    def named(tallies, turn):
        used = int((tallies > 0).sum())
        fixed = max(1, used // 4)
        shifted = fixed + (places - fixed + turn * (used - fixed)) % max(1, amount - fixed)
        return jnp.zeros((amount,), jnp.int32).at[ranking[jnp.where(places < fixed, places, shifted)]].set(jnp.asarray(tallies, jnp.int32))

    tallies = jnp.where(number % 4 == 0, named(packed, number // 4), named(usual, number - number // 4 - 1))
    mixed = jax.random.permutation(jax.random.fold_in(own, 3), amount)
    donor, receiver = mixed[0:amount // 2 * 2:2], mixed[1:amount // 2 * 2:2]
    slack = jnp.minimum(tallies[donor] - 1, limit - tallies[receiver]) // 2
    slack = jnp.where((donor == ranking[0]) | (receiver == ranking[0]) | (tallies[receiver] == 0), 0, jnp.maximum(slack, 0))
    shifted = jax.random.randint(jax.random.fold_in(own, 4), (amount // 2,), 0, 1 << 20) % (slack + 1)
    tallies = tallies.at[donor].add(-shifted).at[receiver].add(shifted)
    items = jnp.searchsorted(jnp.cumsum(tallies), jnp.arange(rows * top), side="right").astype(jnp.int32)
    table = items.reshape(top, rows).T
    table = table[jax.random.permutation(jax.random.fold_in(own, 1), rows)]
    turn = jax.random.randint(jax.random.fold_in(own, 2), (rows, 1), 0, top)
    return jnp.take_along_axis(table, (jnp.arange(top)[None, :] + turn) % top, axis=1)


def portions_of(number_of, total, most, slope, full):
    loads = [(1 << 20) // math.isqrt(grade ** slope) + 1 for grade in range(1, number_of + 1)]
    largest = most if full else min(most, max(-(-total // number_of), total * loads[0] // sum(loads)))
    least = 1 if total - largest >= number_of - 1 else 0
    counts, rest = [largest] + [least] * (number_of - 1), total - largest - least * (number_of - 1)
    while rest > 0:
        movable = [i for i in range(1, number_of) if counts[i] < largest] or [i for i in range(1, number_of) if counts[i] < most]
        pool, left = sum([loads[i] for i in movable]), rest
        for i in movable:
            extra = min(most - counts[i], max(1, left * loads[i] // pool), rest)
            counts[i] = counts[i] + extra
            rest = rest - extra
    return np.array(counts)


def scatter_about(own_key, dims, deviation, limit, pieces=(), kind=jnp.bfloat16):
    drawn = jax.random.normal(own_key, dims, jnp.float32) * deviation
    if len(pieces) > 0:
        drawn = block_scale(own_key, dims, pieces, -0.22, 0.18) * drawn
    return jnp.clip(drawn, min=-limit, max=limit).astype(kind)


def setup_inputs(seed: int = 0) -> dict:
    key_list = jax.random.split(jax.random.key(seed), 8)
    a_tiles = scatter_about(key_list[0], (N_ROW, N_COL * A_DEV, B, B), (B * N_COL * A_DEV // (4 * RT_DEV)) ** -0.5, 0.21875, ((0, 8), (1, 16)))
    a_rows = draw_a_rows(jax.random.fold_in(key_list[7], 71), 0)
    a_cols = plant(jax.random.randint(key_list[2], (N_ROW, N_COL * A_DEV), 0, KT_DEV), jax.random.fold_in(key_list[2], 1), 0, KT_DEV - 1).astype(jnp.int32)
    p_tiles = scatter_about(key_list[3], (N_ROW * P_DEV, N_COL, B, B), 1.0, 6.0, ((0, 8), (1, 16)))
    p_pos = draw_p_pos(jax.random.fold_in(key_list[7], 71), 0)
    r_tiles = scatter_about(key_list[5], (NT, B, B), B ** -0.5, 0.5, ((0, 8),))
    aggregate_keys = jax.random.split(jax.random.fold_in(key_list[6], 1), NT // RT_DEV)
    aggregate_turns = jax.random.permutation(jax.random.fold_in(key_list[6], 3), NT // RT_DEV)
    aggregate = jax.vmap(lambda own, number: deal_out(jax.random.fold_in(key_list[6], 2), own, number, RT_DEV, CT, 1, MOST, 2))(aggregate_keys, aggregate_turns).reshape((NT, 1))
    return {"a_tiles": a_tiles, "a_rows": a_rows, "a_cols": a_cols, "p_tiles": p_tiles, "p_pos": p_pos, "r_tiles": r_tiles, "aggregate": aggregate}


def reference(a_tiles, a_rows, a_cols, p_tiles, p_pos, r_tiles, aggregate):
    positions = p_pos.reshape(N_ROW, P_DEV, N_COL)
    fine_row = jnp.arange(N_ROW, dtype=jnp.int32)[:, None, None] * RT_DEV + positions // CT_DEV
    coarse_col = jnp.arange(N_COL, dtype=jnp.int32)[None, None, :] * CT_DEV + positions % CT_DEV
    stored = p_tiles.reshape(N_ROW, P_DEV, N_COL, B, B).reshape(-1, B, B)
    dense = jnp.zeros((NT, CT, B, B), jnp.bfloat16)
    dense = dense.at[fine_row.reshape(-1), coarse_col.reshape(-1)].set(stored)
    whole_p = jnp.transpose(dense, (0, 2, 1, 3)).reshape(NT, B, NC)

    def one_row(index):
        tiles = a_tiles[index].reshape(N_COL, A_DEV, B, B)
        rows = a_rows[index].reshape(N_COL, A_DEV)
        inner = (jnp.arange(N_COL, dtype=jnp.int32)[:, None] * KT_DEV + a_cols[index].reshape(N_COL, A_DEV)).astype(jnp.int32)

        def step(total, items):
            block_tiles, block_rows, block_inner = items
            taken = whole_p[block_inner]
            terms = jnp.einsum('tab,tbn->tan', block_tiles.astype(jnp.float32), taken.astype(jnp.float32))
            return total.at[block_rows].add(terms), None

        start = jnp.zeros((RT_DEV, B, NC), jnp.float32)
        total, _ = lax.scan(step, start, (tiles, rows, inner))
        return total

    rows_all = lax.map(one_row, jnp.arange(N_ROW, dtype=jnp.int32))
    product = rows_all.reshape(NT, B, NC).astype(jnp.bfloat16)
    contribution = jnp.einsum('tab,tbn->tan', r_tiles.astype(jnp.float32), product.astype(jnp.float32)).astype(jnp.bfloat16)
    coarse = jax.ops.segment_sum(contribution.astype(jnp.float32), aggregate[:, 0], num_segments=CT)
    return product.reshape(N, NC), coarse.reshape(NC, NC)
```

```python
import jax
import jax.numpy as jnp
from jax import lax
from jax.experimental import pallas as pl
from jax.experimental.pallas import tpu as pltpu
from jax.sharding import PartitionSpec as P

MESH = pl.DeviceIdType.MESH

N_A = 48
N_P = 16
N_R = 32
RING = 4
TILES = 8
CHUNKS = N_A // TILES
ROWS = 4
STEPS = N_R // ROWS
NEED = [(min(2 * r, r + N_A - N_R) - 1) // TILES for r in range(ROWS, N_R + 1, ROWS)]


def kernel(
    loc, meta_a, meta_p, a_in, p_in, r_in,
    prod_out, coarse_out,
    a0, a1, a2, a3, land_a, land_p, sib_p, stage, slab,
    s1, r1, s2, r2, prod, cs, cr, xs, xr,
    ma, mp, mq, sma, smp, smq,
    sem_a_s, sem_a_r, sem_p_s, sem_p_r, sem_q_s, sem_q_r,
    sem_ma_s, sem_ma_r, sem_mp_s, sem_mp_r, sem_mq_s, sem_mq_r,
    sem_1_s, sem_1_r, sem_2_s, sem_2_r,
    sem_c_s, sem_c_r, sem_x_s, sem_x_r,
    sem_sma, sem_smp, sem_smq, sem_out,
):
    row, col = lax.axis_index("row"), lax.axis_index("col")
    x, core = lax.div(row, 2), lax.rem(row, 2)
    z, y = lax.div(col, RING), lax.rem(col, RING)

    def at(x_, core_, z_, y_):
        return (x_ * 2 + core_, z_ * RING + y_)

    def turn(v, by):
        return lax.rem(v + by, RING)

    y_dev = [at(x, core, z, turn(y, k)) for k in range(RING)]
    z_dev = [at(x, core, turn(z, k), y) for k in range(RING)]
    x_dev = [at(turn(x, k), core, z, y) for k in range(RING)]
    p_to = [at(turn(x, k), core, x, y) for k in range(RING)]
    p_from = [at(z, core, turn(z, k), y) for k in range(RING)]
    sibling = at(x, 1 - core, z, y)
    keeps = x == z

    def remote(src, dst, send, recv, to):
        return pltpu.make_async_remote_copy(
            src_ref=src, dst_ref=dst, send_sem=send, recv_sem=recv, device_id=to, device_id_type=MESH
        )

    def landed(ref, sem):
        pltpu.make_async_copy(ref, ref, sem).wait()

    barrier = pltpu.get_barrier_semaphore()

    def greet(to):
        pl.semaphore_signal(barrier, inc=1, device_id=to, device_id_type=MESH)

    for to in y_dev[1:] + [z_dev[1], z_dev[3]] + x_dev[1:] + [sibling] + p_to[1:] + p_from[1:]:
        greet(to)

    @pl.when(jnp.logical_not(keeps))
    def _():
        greet(p_to[0])
        greet(p_from[0])

    pl.semaphore_wait(barrier, jnp.where(keeps, 15, 17))

    def p_copy(k):
        d = turn(z - x + RING, 0)
        return (
            remote(p_in, land_p.at[d], sem_p_s.at[k], sem_p_r.at[d], p_to[k]),
            remote(meta_p, mp.at[d], sem_mp_s.at[k], sem_mp_r.at[d], p_to[k]),
        )

    for k in (1, 2, 3):
        for one in p_copy(k):
            one.start()

    @pl.when(jnp.logical_not(keeps))
    def _():
        for one in p_copy(0):
            one.start()

    @pl.when(keeps)
    def _():
        pltpu.make_async_copy(p_in, land_p.at[0], sem_p_r.at[0]).start()
        pltpu.make_async_copy(meta_p, mp.at[0], sem_mp_r.at[0]).start()

    ma_copies = [
        remote(meta_a, ma.at[k], sem_ma_s.at[k], sem_ma_r.at[k], y_dev[to])
        for k, to in ((0, 1), (1, 3), (2, 2))
    ]
    for one in ma_copies:
        one.start()
    pltpu.make_async_copy(meta_a, sma.at[0], sem_sma.at[0]).start()

    everyone = (a0, a1, a2, a3)
    zero = jnp.zeros(a0.shape[1:], a0.dtype)
    for one in everyone:
        one[N_A] = zero

    def sort(s, carry):
        a0[s] = a_in[loc[0, s]]
        return carry

    sent = []

    def send_own(c):
        lax.fori_loop(c * TILES, (c + 1) * TILES, sort, 0, unroll=True)
        part = pl.ds(c * TILES, TILES)
        for kind, to in ((0, 1), (1, 3)):
            one = remote(a0.at[part], land_a.at[kind, part], sem_a_s.at[kind, c], sem_a_r.at[kind, c], y_dev[to])
            one.start()
            sent.append(one)

    half = TILES // 2

    def pass_on(c):
        whole = pl.ds(c * TILES, TILES)
        for kind, to, at_ in ((0, 1, c * TILES), (1, 3, c * TILES + half)):
            landed(land_a.at[kind, whole], sem_a_r.at[kind, c])
            part = pl.ds(at_, half)
            one = remote(
                land_a.at[kind, part], land_a.at[2, part], sem_a_s.at[2 + kind, c], sem_a_r.at[2 + kind, c], y_dev[to]
            )
            one.start()
            sent.append(one)
        if c + 2 < CHUNKS:
            send_own(c + 2)

    def take_in(c):
        for kind, at_ in ((0, c * TILES), (1, c * TILES + half)):
            landed(land_a.at[2, pl.ds(at_, half)], sem_a_r.at[2 + kind, c])

        def move(s, carry):
            a1[s] = land_a[0, s]
            a2[s] = land_a[1, s]
            a3[s] = land_a[2, s]
            return carry

        lax.fori_loop(c * TILES, (c + 1) * TILES, move, 0)

    stage[0, N_P] = zero
    stage[1, N_P] = zero

    def p_pass(d):
        landed(land_p.at[d], sem_p_r.at[d])
        landed(mp.at[d], sem_mp_r.at[d])
        one = remote(mp.at[d], mq.at[d], sem_mq_s.at[d], sem_mq_r.at[d], sibling)
        one.start()
        sent.append(one)
        one = remote(land_p.at[d], sib_p.at[d], sem_q_s.at[d], sem_q_r.at[d], sibling)
        one.start()
        sent.append(one)
        pltpu.make_async_copy(mp.at[d], smp.at[d], sem_smp.at[d]).start()

    def p_slab(d):
        landed(mq.at[d], sem_mq_r.at[d])
        two = pltpu.make_async_copy(mq.at[d], smq.at[d], sem_smq.at[d])
        two.start()
        landed(sib_p.at[d], sem_q_r.at[d])
        for which, (src, table, base) in enumerate(((land_p, smp, core * N_R), (sib_p, smq, (1 - core) * N_R))):
            def move(s, carry):
                stage[which, s] = src[d, s]
                return carry

            lax.fori_loop(0, N_P, move, 0)
            if which == 0:
                pltpu.make_async_copy(mp.at[d], smp.at[d], sem_smp.at[d]).wait()
            else:
                two.wait()

            def place(r, carry):
                slab[d, base + r] = jnp.concatenate(
                    [stage[which, table[d, 0, 2 * r]], stage[which, table[d, 0, 2 * r + 1]]], axis=1
                )
                return carry

            lax.fori_loop(0, N_R, place, 0)

    inner = [turn(y, k) * (2 * N_R // RING) for k in (0, 3, 1, 2)]

    def part(r, d):
        left, right = [], []
        for k in range(4):
            for e in range(2):
                left.append(everyone[k][sma[k, 0, 2 * r + e]])
                right.append(slab[d, inner[k] + sma[k, 1, 2 * r + e]])
        return jnp.dot(
            jnp.concatenate(left, axis=1), jnp.concatenate(right, axis=0), preferred_element_type=jnp.float32
        )

    def first(q):
        def body(i, carry):
            s1[q, i] = part(q * ROWS + i, 2).astype(s1.dtype)
            return carry

        lax.fori_loop(0, ROWS, body, 0)
        for kind, to in ((0, 1), (1, 3)):
            one = remote(
                s1.at[q, pl.ds(kind * (ROWS // 2), ROWS // 2)], r1.at[q, kind], sem_1_s.at[q, kind], sem_1_r.at[q, kind], z_dev[to]
            )
            one.start()
            sent.append(one)

    def second(q):
        for kind, to in ((0, 1), (1, 3)):
            lo = kind * (ROWS // 2)

            def plain(i, carry):
                s2[q, kind, i] = part(q * ROWS + i, to).astype(s2.dtype)
                return carry

            def added(i, carry):
                s2[q, kind, lo + i] = (part(q * ROWS + lo + i, to) + r1[q, kind, i].astype(jnp.float32)).astype(s2.dtype)
                return carry

            other = ROWS // 2 - lo
            lax.fori_loop(other, other + ROWS // 2, plain, 0)
            landed(r1.at[q, kind], sem_1_r.at[q, kind])
            lax.fori_loop(0, ROWS // 2, added, 0)
            one = remote(s2.at[q, kind], r2.at[q, kind], sem_2_s.at[q, kind], sem_2_r.at[q, kind], z_dev[to])
            one.start()
            sent.append(one)

    outs = []

    def third(q):
        for kind in range(2):
            landed(r2.at[q, kind], sem_2_r.at[q, kind])

        def body(i, carry):
            total = part(q * ROWS + i, 0) + r2[q, 0, i].astype(jnp.float32) + r2[q, 1, i].astype(jnp.float32)
            prod[q * ROWS + i] = total.astype(prod.dtype)
            return carry

        lax.fori_loop(0, ROWS, body, 0)
        one = pltpu.make_async_copy(prod.at[pl.ds(q * ROWS, ROWS)], prod_out.at[pl.ds(q * ROWS, ROWS)], sem_out.at[q])
        one.start()
        outs.append(one)

    prod[N_R] = jnp.zeros(prod.shape[1:], prod.dtype)

    send_own(0)
    send_own(1)
    pass_on(0)
    pass_on(1)
    for d in (2, 1, 3, 0):
        p_pass(d)
    for k in range(3):
        landed(ma.at[k], sem_ma_r.at[k])
        pltpu.make_async_copy(ma.at[k], sma.at[k + 1], sem_sma.at[k + 1]).start()
    take_in(0)
    pltpu.make_async_copy(meta_a, sma.at[0], sem_sma.at[0]).wait()
    for k in range(3):
        pltpu.make_async_copy(ma.at[k], sma.at[k + 1], sem_sma.at[k + 1]).wait()
    p_slab(2)
    have = 0
    for q in range(STEPS + 2):
        if q < STEPS:
            while have < NEED[q]:
                have += 1
                take_in(have)
            first(q)
            if q + 2 < CHUNKS:
                pass_on(q + 2)
        if q == 0:
            p_slab(1)
            p_slab(3)
        if 1 <= q <= STEPS:
            second(q - 1)
        if q == 1:
            p_slab(0)
        if q >= 2:
            third(q - 2)

    def coarse(c):
        t0, t1 = loc[1, 2 * c], loc[1, 2 * c + 1]
        u0, u1 = loc[2, 2 * c], loc[2, 2 * c + 1]
        return jnp.dot(
            jnp.concatenate([r_in[u0], r_in[u1]], axis=1),
            jnp.concatenate([prod[t0], prod[t1]], axis=0),
            preferred_element_type=jnp.float32,
        )

    order = (2, 1, 3, 0)
    for s in order:
        base = turn(x, s) * 8 + (1 - core) * 4

        def body(u, carry):
            cs[s, u] = coarse(base + u).astype(cs.dtype)
            return carry

        lax.fori_loop(0, 4, body, 0)
        one = remote(cs.at[s], cr.at[s], sem_c_s.at[s], sem_c_r.at[s], sibling)
        one.start()
        sent.append(one)
    for s in order:
        base = turn(x, s) * 8 + core * 4
        landed(cr.at[s], sem_c_r.at[s])

        def body(u, carry):
            total = coarse(base + u) + cr[s, u].astype(jnp.float32)
            if s == 0:
                coarse_out[u] = total
            else:
                xs[s - 1, u] = total.astype(xs.dtype)
            return carry

        lax.fori_loop(0, 4, body, 0)
        if s > 0:
            one = remote(xs.at[s - 1], xr.at[s - 1], sem_x_s.at[s - 1], sem_x_r.at[s - 1], x_dev[s])
            one.start()
            sent.append(one)
    for s in (1, 3, 2):
        landed(xr.at[s - 1], sem_x_r.at[s - 1])

    def body(u, carry):
        total = coarse_out[u]
        for s in range(3):
            total = total + xr[s, u].astype(jnp.float32)
        coarse_out[u] = total
        return carry

    lax.fori_loop(0, 4, body, 0)

    for one in sent + ma_copies:
        one.wait_send()
    for k in (1, 2, 3):
        for one in p_copy(k):
            one.wait_send()

    @pl.when(jnp.logical_not(keeps))
    def _():
        for one in p_copy(0):
            one.wait_send()

    for one in outs:
        one.wait()


def tables(a_rows, a_cols, p_pos, aggregate):
    def lanes(v, fill):
        return jnp.concatenate([v, jnp.full((128 - v.shape[0],), fill, jnp.int32)])

    def spread(index, value, fill):
        hit = index[:, None] == jnp.arange(128, dtype=jnp.int32)[None, :]
        return fill + jnp.sum(jnp.where(hit, (value - fill)[:, None], 0), axis=0)

    def earlier(v):
        n = jnp.arange(v.shape[0], dtype=jnp.int32)
        return (v[None, :] == v[:, None]) & (n[None, :] < n[:, None])

    same = earlier(a_rows)
    rank = jnp.sum(((a_rows[None, :] < a_rows[:, None]) | same).astype(jnp.int32), axis=1)
    slot = a_rows * 2 + jnp.sum(same.astype(jnp.int32), axis=1)
    perm = spread(rank, jnp.arange(N_A, dtype=jnp.int32), 0)
    pos = spread(slot, rank, N_A)
    inner = spread(slot, a_cols, 0)
    stored = spread(p_pos, jnp.arange(N_P, dtype=jnp.int32), N_P)
    named = aggregate * 2 + jnp.sum(earlier(aggregate).astype(jnp.int32), axis=1)
    fine = spread(named, jnp.arange(N_R, dtype=jnp.int32), N_R)
    none = jnp.zeros((128,), jnp.int32)
    loc = jnp.stack([perm, fine, jnp.minimum(fine, N_R - 1)] + [none] * 5)
    meta_a = jnp.stack([pos, inner] + [none] * 6)
    meta_p = jnp.stack([stored] + [none] * 7)
    return loc, meta_a, meta_p


def local(a_tiles, a_rows, a_cols, p_tiles, p_pos, r_tiles, aggregate):
    b = a_tiles.shape[-1]
    band = 2 * b
    loc, meta_a, meta_p = tables(a_rows[0], a_cols[0], p_pos[:, 0], aggregate[:, 0])
    bf, f32, i32 = jnp.bfloat16, jnp.float32, jnp.int32
    vmem, smem, dma = pltpu.VMEM, pltpu.SMEM, pltpu.SemaphoreType.DMA
    scratch = (
        [vmem((N_A + 1, b, b), bf)] * 4
        + [
            vmem((3, N_A, b, b), bf),
            vmem((4, N_P, b, b), bf),
            vmem((4, N_P, b, b), bf),
            vmem((2, N_P + 1, b, b), bf),
            vmem((4, 2 * N_R, b, band), bf),
            vmem((STEPS, ROWS, b, band), bf),
            vmem((STEPS, 2, ROWS // 2, b, band), bf),
            vmem((STEPS, 2, ROWS, b, band), bf),
            vmem((STEPS, 2, ROWS, b, band), bf),
            vmem((N_R + 1, b, band), bf),
            vmem((4, 4, b, band), bf),
            vmem((4, 4, b, band), bf),
            vmem((3, 4, b, band), bf),
            vmem((3, 4, b, band), bf),
            vmem((3, 8, 128), i32),
            vmem((4, 8, 128), i32),
            vmem((4, 8, 128), i32),
            smem((4, 8, 128), i32),
            smem((4, 8, 128), i32),
            smem((4, 8, 128), i32),
        ]
        + [dma((4, CHUNKS)), dma((4, CHUNKS))]
        + [dma((4,))] * 4
        + [dma((3,))] * 2
        + [dma((4,))] * 4
        + [dma((STEPS, 2))] * 4
        + [dma((4,))] * 2
        + [dma((3,))] * 2
        + [dma((4,)), dma((4,)), dma((4,)), dma((STEPS,))]
    )
    in_vmem = pl.BlockSpec(memory_space=pltpu.VMEM)
    anywhere = pl.BlockSpec(memory_space=pl.ANY)
    product, coarse = pl.pallas_call(
        kernel,
        out_shape=(
            jax.ShapeDtypeStruct((N_R, b, band), bf),
            jax.ShapeDtypeStruct((4, b, band), f32),
        ),
        in_specs=[pl.BlockSpec(memory_space=pltpu.SMEM), in_vmem, in_vmem, in_vmem, anywhere, in_vmem],
        out_specs=(anywhere, in_vmem),
        scratch_shapes=scratch,
        compiler_params=pltpu.CompilerParams(
            collective_id=0, has_side_effects=True, vmem_limit_bytes=60 * 1024 * 1024
        ),
        cost_estimate=pl.CostEstimate(flops=9 * 10**9, bytes_accessed=10**7, transcendentals=0),
    )(loc, meta_a, meta_p, a_tiles[0], p_tiles[:, 0], r_tiles)
    return product.reshape(N_R * b, band), coarse.reshape(4 * b, band)


def solution(mesh):
    in_specs = (
        P("row", "col", None, None),
        P("row", "col"),
        P("row", "col"),
        P("row", "col", None, None),
        P("row", "col"),
        P("row", None, None),
        P("row", None),
    )
    out_specs = (P("row", "col"), P("row", "col"))
    return jax.shard_map(local, mesh=mesh, in_specs=in_specs, out_specs=out_specs, check_vma=False)
```

```python
import jax
import jax.numpy as jnp
from jax import lax
from jax.experimental import pallas as pl
from jax.experimental.pallas import tpu as pltpu
from jax.sharding import PartitionSpec as P

MESH = pl.DeviceIdType.MESH

N_A = 48
N_P = 16
N_R = 32
RING = 4
TILES = 8
CHUNKS = N_A // TILES
ROWS = 4
STEPS = N_R // ROWS
NEED = [(min(2 * r, r + N_A - N_R) - 1) // TILES for r in range(ROWS, N_R + 1, ROWS)]


def kernel(
    loc, meta_a, meta_p, a_in, p_in, r_in,
    prod_out, coarse_out,
    a0, a1, a2, a3, land_a, pg, sg, stage, slab,
    s1, r1, s2, r2, prod, cs, cr, xs, xr,
    ma, mp, mq, sma, smp, smq,
    sem_a_s, sem_a_r, sem_p_s, sem_p_r, sem_g_s, sem_g_r, sem_q_s, sem_q_r,
    sem_ma_s, sem_ma_r, sem_mp_s, sem_mp_r, sem_mq_s, sem_mq_r,
    sem_1_s, sem_1_r, sem_2_s, sem_2_r,
    sem_c_s, sem_c_r, sem_x_s, sem_x_r,
    sem_sma, sem_smp, sem_smq, sem_out,
):
    row, col = lax.axis_index("row"), lax.axis_index("col")
    x, core = lax.div(row, 2), lax.rem(row, 2)
    z, y = lax.div(col, RING), lax.rem(col, RING)

    def at(x_, core_, z_, y_):
        return (x_ * 2 + core_, z_ * RING + y_)

    def turn(v, by):
        return lax.rem(v + by, RING)

    y_dev = [at(x, core, z, turn(y, k)) for k in range(RING)]
    z_dev = [at(x, core, turn(z, k), y) for k in range(RING)]
    x_dev = [at(turn(x, k), core, z, y) for k in range(RING)]
    p_to = [at(turn(x, k), core, x, y) for k in range(RING)]
    p_from = [at(z, core, turn(z, k), y) for k in range(RING)]
    sibling = at(x, 1 - core, z, y)
    keeps = x == z

    def remote(src, dst, send, recv, to):
        return pltpu.make_async_remote_copy(
            src_ref=src, dst_ref=dst, send_sem=send, recv_sem=recv, device_id=to, device_id_type=MESH
        )

    def landed(ref, sem):
        pltpu.make_async_copy(ref, ref, sem).wait()

    barrier = pltpu.get_barrier_semaphore()

    def greet(to):
        pl.semaphore_signal(barrier, inc=1, device_id=to, device_id_type=MESH)

    for to in y_dev[1:] + [z_dev[1], z_dev[3]] + x_dev[1:] + [sibling] + p_to[1:] + p_from[1:]:
        greet(to)

    @pl.when(jnp.logical_not(keeps))
    def _():
        greet(p_to[0])
        greet(p_from[0])

    pl.semaphore_wait(barrier, jnp.where(keeps, 15, 17))

    quarter = N_P // RING

    def p_copy(k):
        d = turn(z - x + RING, 0)
        return (
            remote(p_in.at[pl.ds(k * quarter, quarter)], pg.at[0, d], sem_p_s.at[k], sem_p_r.at[d], p_to[k]),
            remote(meta_p, mp.at[d], sem_mp_s.at[k], sem_mp_r.at[d], p_to[k]),
        )

    for k in (1, 2, 3):
        for one in p_copy(k):
            one.start()

    @pl.when(jnp.logical_not(keeps))
    def _():
        for one in p_copy(0):
            one.start()

    @pl.when(keeps)
    def _():
        pltpu.make_async_copy(p_in.at[pl.ds(0, quarter)], pg.at[0, 0], sem_p_r.at[0]).start()
        pltpu.make_async_copy(meta_p, mp.at[0], sem_mp_r.at[0]).start()

    ma_copies = [
        remote(meta_a, ma.at[k], sem_ma_s.at[k], sem_ma_r.at[k], y_dev[to])
        for k, to in ((0, 1), (1, 3), (2, 2))
    ]
    for one in ma_copies:
        one.start()
    pltpu.make_async_copy(meta_a, sma.at[0], sem_sma.at[0]).start()

    everyone = (a0, a1, a2, a3)
    zero = jnp.zeros(a0.shape[1:], a0.dtype)
    for one in everyone:
        one[N_A] = zero

    def sort(s, carry):
        a0[s] = a_in[loc[0, s]]
        return carry

    sent = []

    def send_own(c):
        lax.fori_loop(c * TILES, (c + 1) * TILES, sort, 0, unroll=True)
        part = pl.ds(c * TILES, TILES)
        for kind, to in ((0, 1), (1, 3)):
            one = remote(a0.at[part], land_a.at[kind, part], sem_a_s.at[kind, c], sem_a_r.at[kind, c], y_dev[to])
            one.start()
            sent.append(one)

    half = TILES // 2

    def pass_on(c):
        whole = pl.ds(c * TILES, TILES)
        for kind, to, at_ in ((0, 1, c * TILES), (1, 3, c * TILES + half)):
            landed(land_a.at[kind, whole], sem_a_r.at[kind, c])
            part = pl.ds(at_, half)
            one = remote(
                land_a.at[kind, part], land_a.at[2, part], sem_a_s.at[2 + kind, c], sem_a_r.at[2 + kind, c], y_dev[to]
            )
            one.start()
            sent.append(one)
        if c + 3 < CHUNKS:
            send_own(c + 3)

    def take_in(c):
        for kind, at_ in ((0, c * TILES), (1, c * TILES + half)):
            landed(land_a.at[2, pl.ds(at_, half)], sem_a_r.at[2 + kind, c])

        def move(s, carry):
            a1[s] = land_a[0, s]
            a2[s] = land_a[1, s]
            a3[s] = land_a[2, s]
            return carry

        lax.fori_loop(c * TILES, (c + 1) * TILES, move, 0, unroll=2)

    stage[0, N_P] = zero
    stage[1, N_P] = zero

    def to_core(kind, d):
        one = remote(pg.at[kind, d], sg.at[kind, d], sem_q_s.at[kind, d], sem_q_r.at[kind, d], sibling)
        one.start()
        sent.append(one)

    def p_start(d):
        landed(pg.at[0, d], sem_p_r.at[d])
        for kind, to in ((1, 1), (2, 3)):
            one = remote(pg.at[0, d], pg.at[kind, d], sem_g_s.at[kind - 1, d], sem_g_r.at[kind - 1, d], x_dev[to])
            one.start()
            sent.append(one)
        to_core(0, d)
        landed(mp.at[d], sem_mp_r.at[d])
        one = remote(mp.at[d], mq.at[d], sem_mq_s.at[d], sem_mq_r.at[d], sibling)
        one.start()
        sent.append(one)
        pltpu.make_async_copy(mp.at[d], smp.at[d], sem_smp.at[d]).start()

    def p_pass(d):
        for kind, to, at_ in ((1, 1, 0), (2, 3, quarter // 2)):
            landed(pg.at[kind, d], sem_g_r.at[kind - 1, d])
            two = pl.ds(at_, quarter // 2)
            one = remote(
                pg.at[kind, d, two], pg.at[3, d, two], sem_g_s.at[1 + kind, d], sem_g_r.at[1 + kind, d], x_dev[to]
            )
            one.start()
            sent.append(one)
        for kind in (1, 2):
            to_core(kind, d)

    def p_done(d):
        for kind, at_ in ((1, 0), (2, quarter // 2)):
            landed(pg.at[3, d, pl.ds(at_, quarter // 2)], sem_g_r.at[1 + kind, d])
        to_core(3, d)

    quarters = [turn(x - z + RING, k) * quarter for k in (0, 3, 1, 2)]

    def p_slab(d):
        landed(mq.at[d], sem_mq_r.at[d])
        two = pltpu.make_async_copy(mq.at[d], smq.at[d], sem_smq.at[d])
        two.start()
        for which, (src, table, base) in enumerate(((pg, smp, core * N_R), (sg, smq, (1 - core) * N_R))):
            for kind in range(4):
                if which:
                    landed(sg.at[kind, d], sem_q_r.at[kind, d])

                def move(s, carry):
                    stage[which, quarters[kind] + s] = src[kind, d, s]
                    return carry

                lax.fori_loop(0, quarter, move, 0, unroll=True)
            if which == 0:
                pltpu.make_async_copy(mp.at[d], smp.at[d], sem_smp.at[d]).wait()
            else:
                two.wait()

            def place(r, carry):
                slab[d, base + r] = jnp.concatenate(
                    [stage[which, table[d, 0, 2 * r]], stage[which, table[d, 0, 2 * r + 1]]], axis=1
                )
                return carry

            lax.fori_loop(0, N_R, place, 0, unroll=4)

    inner = [turn(y, k) * (2 * N_R // RING) for k in (0, 3, 1, 2)]

    def part(r, d):
        left, right = [], []
        for k in range(4):
            for e in range(2):
                left.append(everyone[k][sma[k, 0, 2 * r + e]])
                right.append(slab[d, inner[k] + sma[k, 1, 2 * r + e]])
        return jnp.dot(
            jnp.concatenate(left, axis=1), jnp.concatenate(right, axis=0), preferred_element_type=jnp.float32
        )

    def first(q):
        def body(i, carry):
            s1[q, i] = part(q * ROWS + i, 2).astype(s1.dtype)
            return carry

        lax.fori_loop(0, ROWS, body, 0, unroll=True)
        for kind, to in ((0, 1), (1, 3)):
            one = remote(
                s1.at[q, pl.ds(kind * (ROWS // 2), ROWS // 2)], r1.at[q, kind], sem_1_s.at[q, kind], sem_1_r.at[q, kind], z_dev[to]
            )
            one.start()
            sent.append(one)

    def second(q):
        for kind, to in ((0, 1), (1, 3)):
            lo = kind * (ROWS // 2)

            def plain(i, carry):
                s2[q, kind, i] = part(q * ROWS + i, to).astype(s2.dtype)
                return carry

            def added(i, carry):
                s2[q, kind, lo + i] = (part(q * ROWS + lo + i, to) + r1[q, kind, i].astype(jnp.float32)).astype(s2.dtype)
                return carry

            other = ROWS // 2 - lo
            lax.fori_loop(other, other + ROWS // 2, plain, 0, unroll=True)
            landed(r1.at[q, kind], sem_1_r.at[q, kind])
            lax.fori_loop(0, ROWS // 2, added, 0, unroll=True)
            one = remote(s2.at[q, kind], r2.at[q, kind], sem_2_s.at[q, kind], sem_2_r.at[q, kind], z_dev[to])
            one.start()
            sent.append(one)

    outs = []

    def third(q):
        for kind in range(2):
            landed(r2.at[q, kind], sem_2_r.at[q, kind])

        def body(i, carry):
            total = part(q * ROWS + i, 0) + r2[q, 0, i].astype(jnp.float32) + r2[q, 1, i].astype(jnp.float32)
            prod[q * ROWS + i] = total.astype(prod.dtype)
            return carry

        lax.fori_loop(0, ROWS, body, 0, unroll=True)
        one = pltpu.make_async_copy(prod.at[pl.ds(q * ROWS, ROWS)], prod_out.at[pl.ds(q * ROWS, ROWS)], sem_out.at[q])
        one.start()
        outs.append(one)

    prod[N_R] = jnp.zeros(prod.shape[1:], prod.dtype)

    for c in range(3):
        send_own(c)
    for d in (2, 1, 3, 0):
        p_start(d)
    pass_on(0)
    p_pass(2)
    p_pass(1)
    p_done(2)
    p_pass(3)
    p_done(1)
    for k in range(3):
        landed(ma.at[k], sem_ma_r.at[k])
        pltpu.make_async_copy(ma.at[k], sma.at[k + 1], sem_sma.at[k + 1]).start()
    take_in(0)
    pltpu.make_async_copy(meta_a, sma.at[0], sem_sma.at[0]).wait()
    for k in range(3):
        pltpu.make_async_copy(ma.at[k], sma.at[k + 1], sem_sma.at[k + 1]).wait()
    p_slab(2)
    have = 0
    for q in range(STEPS + 2):
        if q < STEPS:
            while have < NEED[q]:
                have += 1
                take_in(have)
            first(q)
            if q + 1 < CHUNKS:
                pass_on(q + 1)
        if q == 0:
            p_pass(0)
            p_done(3)
            p_slab(1)
            p_slab(3)
        if 1 <= q <= STEPS:
            second(q - 1)
        if q == 1:
            p_done(0)
            p_slab(0)
        if q >= 2:
            third(q - 2)

    def coarse(c):
        t0, t1 = loc[1, 2 * c], loc[1, 2 * c + 1]
        u0, u1 = loc[2, 2 * c], loc[2, 2 * c + 1]
        return jnp.dot(
            jnp.concatenate([r_in[u0], r_in[u1]], axis=1),
            jnp.concatenate([prod[t0], prod[t1]], axis=0),
            preferred_element_type=jnp.float32,
        )

    order = (2, 1, 3, 0)
    for s in order:
        base = turn(x, s) * 8 + (1 - core) * 4

        def body(u, carry):
            cs[s, u] = coarse(base + u).astype(cs.dtype)
            return carry

        lax.fori_loop(0, 4, body, 0, unroll=True)
        one = remote(cs.at[s], cr.at[s], sem_c_s.at[s], sem_c_r.at[s], sibling)
        one.start()
        sent.append(one)
    for s in order:
        base = turn(x, s) * 8 + core * 4
        landed(cr.at[s], sem_c_r.at[s])

        def body(u, carry):
            total = coarse(base + u) + cr[s, u].astype(jnp.float32)
            if s == 0:
                coarse_out[u] = total
            else:
                xs[s - 1, u] = total.astype(xs.dtype)
            return carry

        lax.fori_loop(0, 4, body, 0, unroll=True)
        if s > 0:
            one = remote(xs.at[s - 1], xr.at[s - 1], sem_x_s.at[s - 1], sem_x_r.at[s - 1], x_dev[s])
            one.start()
            sent.append(one)
    for s in (1, 3, 2):
        landed(xr.at[s - 1], sem_x_r.at[s - 1])

    def body(u, carry):
        total = coarse_out[u]
        for s in range(3):
            total = total + xr[s, u].astype(jnp.float32)
        coarse_out[u] = total
        return carry

    lax.fori_loop(0, 4, body, 0)

    for one in sent + ma_copies:
        one.wait_send()
    for k in (1, 2, 3):
        for one in p_copy(k):
            one.wait_send()

    @pl.when(jnp.logical_not(keeps))
    def _():
        for one in p_copy(0):
            one.wait_send()

    for one in outs:
        one.wait()


def tables(a_rows, a_cols, p_pos, aggregate, loc, meta_a, meta_p):
    shape = (128, 128)
    down = lax.broadcasted_iota(jnp.int32, shape, 0).astype(jnp.float32)
    along = lax.broadcasted_iota(jnp.int32, shape, 1).astype(jnp.float32)
    far = 1000.0

    def lanes(v):
        v = jnp.concatenate([v.astype(jnp.float32), jnp.full((1, 128 - v.shape[1]), far, jnp.float32)], axis=1)
        return jnp.broadcast_to(v, shape)

    def rows(v):
        v = jnp.concatenate([v.astype(jnp.float32), jnp.full((128 - v.shape[0], 1), far, jnp.float32)], axis=0)
        return jnp.broadcast_to(v, shape)

    def count(hit, axis):
        return jnp.sum(jnp.where(hit, 1.0, 0.0), axis=axis, keepdims=True)

    def spread(index, value, fill):
        return fill + jnp.sum(jnp.where(index == along, value - fill, 0.0), axis=0, keepdims=True)

    here = lanes(a_rows[...])
    there = here.T
    same = (here == there) & (along < down)
    rank = count((here < there) | same, 1)
    slot = there * 2.0 + count(same, 1)
    perm = spread(rank, down, 0.0)
    pos = spread(slot, rank, float(N_A))
    inner = spread(slot, lanes(a_cols[...]).T, 0.0)
    stored = spread(rows(p_pos[...]), down, float(N_P))
    named = rows(aggregate[...])
    fine = spread(named * 2.0 + count((named == named.T) & (along < down), 1), down, float(N_R))
    none = jnp.zeros((1, 128), jnp.float32)

    def pack(*lines):
        return jnp.concatenate(list(lines) + [none] * (8 - len(lines)), axis=0).astype(jnp.int32)

    loc[...] = pack(perm, fine, jnp.minimum(fine, N_R - 1.0))
    meta_a[...] = pack(pos, inner)
    meta_p[...] = pack(stored)


def local(a_tiles, a_rows, a_cols, p_tiles, p_pos, r_tiles, aggregate):
    b = a_tiles.shape[-1]
    band = 2 * b
    loc, meta_a, meta_p = pl.pallas_call(
        tables, out_shape=(jax.ShapeDtypeStruct((8, 128), jnp.int32),) * 3
    )(a_rows, a_cols, p_pos, aggregate)
    bf, f32, i32 = jnp.bfloat16, jnp.float32, jnp.int32
    vmem, smem, dma = pltpu.VMEM, pltpu.SMEM, pltpu.SemaphoreType.DMA
    scratch = (
        [vmem((N_A + 1, b, b), bf)] * 4
        + [
            vmem((3, N_A, b, b), bf),
            vmem((4, 4, N_P // RING, b, b), bf),
            vmem((4, 4, N_P // RING, b, b), bf),
            vmem((2, N_P + 1, b, b), bf),
            vmem((4, 2 * N_R, b, band), bf),
            vmem((STEPS, ROWS, b, band), bf),
            vmem((STEPS, 2, ROWS // 2, b, band), bf),
            vmem((STEPS, 2, ROWS, b, band), bf),
            vmem((STEPS, 2, ROWS, b, band), bf),
            vmem((N_R + 1, b, band), bf),
            vmem((4, 4, b, band), bf),
            vmem((4, 4, b, band), bf),
            vmem((3, 4, b, band), bf),
            vmem((3, 4, b, band), bf),
            vmem((3, 8, 128), i32),
            vmem((4, 8, 128), i32),
            vmem((4, 8, 128), i32),
            smem((4, 8, 128), i32),
            smem((4, 8, 128), i32),
            smem((4, 8, 128), i32),
        ]
        + [dma((4, CHUNKS)), dma((4, CHUNKS))]
        + [dma((4,))] * 2
        + [dma((4, 4))] * 4
        + [dma((3,))] * 2
        + [dma((4,))] * 4
        + [dma((STEPS, 2))] * 4
        + [dma((4,))] * 2
        + [dma((3,))] * 2
        + [dma((4,)), dma((4,)), dma((4,)), dma((STEPS,))]
    )
    in_vmem = pl.BlockSpec(memory_space=pltpu.VMEM)
    anywhere = pl.BlockSpec(memory_space=pl.ANY)
    product, coarse = pl.pallas_call(
        kernel,
        out_shape=(
            jax.ShapeDtypeStruct((N_R, b, band), bf),
            jax.ShapeDtypeStruct((4, b, band), f32),
        ),
        in_specs=[pl.BlockSpec(memory_space=pltpu.SMEM), in_vmem, in_vmem, in_vmem, anywhere, in_vmem],
        out_specs=(anywhere, in_vmem),
        scratch_shapes=scratch,
        compiler_params=pltpu.CompilerParams(
            collective_id=0, has_side_effects=True, vmem_limit_bytes=60 * 1024 * 1024
        ),
        cost_estimate=pl.CostEstimate(flops=9 * 10**9, bytes_accessed=10**7, transcendentals=0),
    )(loc, meta_a, meta_p, a_tiles[0], p_tiles[:, 0], r_tiles)
    return product.reshape(N_R * b, band), coarse.reshape(4 * b, band)


def solution(mesh):
    in_specs = (
        P("row", "col", None, None),
        P("row", "col"),
        P("row", "col"),
        P("row", "col", None, None),
        P("row", "col"),
        P("row", None, None),
        P("row", None),
    )
    out_specs = (P("row", "col"), P("row", "col"))
    return jax.shard_map(local, mesh=mesh, in_specs=in_specs, out_specs=out_specs, check_vma=False)
```

```python
import jax
import jax.numpy as jnp
from jax import lax
from jax.experimental import pallas as pl
from jax.experimental.pallas import tpu as pltpu
from jax.sharding import PartitionSpec as P

MESH = pl.DeviceIdType.MESH

N_A = 48
N_P = 16
N_R = 32
RING = 4
TILES = 8
CHUNKS = N_A // TILES
UNITS = [(0, 4, None), (4, 4, None), (8, 4, None), (12, 4, None), (16, 8, 0), (24, 8, 0), (16, 8, 1), (24, 8, 1)]
STEPS = len(UNITS)
PARTS = 8
NEED = [(min(2 * (r + n), r + n + N_A - N_R) - 1) // TILES for r, n, _ in UNITS]


def kernel(
    loc, meta_a, meta_p, a_hbm, p_in, r_hbm,
    prod_out, coarse_out,
    a_in, r_in, a0, a1, a2, a3, land_a, pg, sg, stage, slab,
    s1, r1, s2, r2, prod, cs, cr, xs, xr,
    ma, mp, mq, sma, smp, smq,
    sem_a_s, sem_a_r, sem_p_s, sem_p_r, sem_g_s, sem_g_r, sem_q_s, sem_q_r,
    sem_ma_s, sem_ma_r, sem_mp_s, sem_mp_r, sem_mq_s, sem_mq_r,
    sem_1_s, sem_1_r, sem_2_s, sem_2_r,
    sem_c_s, sem_c_r, sem_x_s, sem_x_r,
    sem_sma, sem_smp, sem_smq, sem_out, sem_in,
):
    row, col = lax.axis_index("row"), lax.axis_index("col")
    x, core = lax.div(row, 2), lax.rem(row, 2)
    z, y = lax.div(col, RING), lax.rem(col, RING)

    def at(x_, core_, z_, y_):
        return (x_ * 2 + core_, z_ * RING + y_)

    def turn(v, by):
        return lax.rem(v + by, RING)

    y_dev = [at(x, core, z, turn(y, k)) for k in range(RING)]
    z_dev = [at(x, core, turn(z, k), y) for k in range(RING)]
    x_dev = [at(turn(x, k), core, z, y) for k in range(RING)]
    p_to = [at(turn(x, k), core, x, y) for k in range(RING)]
    p_from = [at(z, core, turn(z, k), y) for k in range(RING)]
    sibling = at(x, 1 - core, z, y)
    keeps = x == z

    a_load = pltpu.make_async_copy(a_hbm, a_in, sem_in.at[0])
    r_load = pltpu.make_async_copy(r_hbm, r_in, sem_in.at[1])
    a_load.start()
    r_load.start()

    def remote(src, dst, send, recv, to):
        return pltpu.make_async_remote_copy(
            src_ref=src, dst_ref=dst, send_sem=send, recv_sem=recv, device_id=to, device_id_type=MESH
        )

    def landed(ref, sem):
        pltpu.make_async_copy(ref, ref, sem).wait()

    barrier = pltpu.get_barrier_semaphore()

    def greet(to):
        pl.semaphore_signal(barrier, inc=1, device_id=to, device_id_type=MESH)

    for to in y_dev[1:] + [z_dev[1], z_dev[3]] + x_dev[1:] + [sibling] + p_to[1:] + p_from[1:]:
        greet(to)

    @pl.when(jnp.logical_not(keeps))
    def _():
        greet(p_to[0])
        greet(p_from[0])

    pltpu.make_async_copy(meta_a, sma.at[0], sem_sma.at[0]).start()
    everyone = (a0, a1, a2, a3)
    zero = jnp.zeros(a0.shape[1:], a0.dtype)
    for one in everyone:
        one[N_A] = zero
    stage[0, N_P] = zero
    stage[1, N_P] = zero
    prod[0, N_R] = zero
    prod[1, N_R] = zero
    a_load.wait()

    def sort(s, carry):
        a0[s] = a_in[loc[0, s]]
        return carry

    lax.fori_loop(0, 3 * TILES, sort, 0, unroll=4)
    pl.semaphore_wait(barrier, jnp.where(keeps, 15, 17))

    quarter = N_P // RING

    def p_copy(k):
        d = turn(z - x + RING, 0)
        return (
            remote(p_in.at[pl.ds(k * quarter, quarter)], pg.at[0, d], sem_p_s.at[k], sem_p_r.at[d], p_to[k]),
            remote(meta_p, mp.at[d], sem_mp_s.at[k], sem_mp_r.at[d], p_to[k]),
        )

    for k in (1, 2, 3):
        for one in p_copy(k):
            one.start()

    @pl.when(jnp.logical_not(keeps))
    def _():
        for one in p_copy(0):
            one.start()

    @pl.when(keeps)
    def _():
        pltpu.make_async_copy(p_in.at[pl.ds(0, quarter)], pg.at[0, 0], sem_p_r.at[0]).start()
        pltpu.make_async_copy(meta_p, mp.at[0], sem_mp_r.at[0]).start()

    ma_copies = [
        remote(meta_a, ma.at[k], sem_ma_s.at[k], sem_ma_r.at[k], y_dev[to])
        for k, to in ((0, 1), (1, 3), (2, 2))
    ]
    for one in ma_copies:
        one.start()
    sent = []

    def send_own(c):
        part = pl.ds(c * TILES, TILES)
        for kind, to in ((0, 1), (1, 3)):
            one = remote(a0.at[part], land_a.at[kind, part], sem_a_s.at[kind, c], sem_a_r.at[kind, c], y_dev[to])
            one.start()
            sent.append(one)

    half = TILES // 2

    def pass_on(c):
        whole = pl.ds(c * TILES, TILES)
        for kind, to, at_ in ((0, 1, c * TILES), (1, 3, c * TILES + half)):
            landed(land_a.at[kind, whole], sem_a_r.at[kind, c])
            part = pl.ds(at_, half)
            one = remote(
                land_a.at[kind, part], land_a.at[2, part], sem_a_s.at[2 + kind, c], sem_a_r.at[2 + kind, c], y_dev[to]
            )
            one.start()
            sent.append(one)
        if c + 2 < CHUNKS:
            send_own(c + 2)

    def take_in(c):
        for kind, at_ in ((0, c * TILES), (1, c * TILES + half)):
            landed(land_a.at[2, pl.ds(at_, half)], sem_a_r.at[2 + kind, c])

        def move(s, carry):
            a1[s] = land_a[0, s]
            a2[s] = land_a[1, s]
            a3[s] = land_a[2, s]
            return carry

        lax.fori_loop(c * TILES, (c + 1) * TILES, move, 0, unroll=2)

    def to_core(kind, d):
        one = remote(pg.at[kind, d], sg.at[kind, d], sem_q_s.at[kind, d], sem_q_r.at[kind, d], sibling)
        one.start()
        sent.append(one)

    def p_start(d):
        landed(pg.at[0, d], sem_p_r.at[d])
        for kind, to in ((1, 1), (2, 3)):
            one = remote(pg.at[0, d], pg.at[kind, d], sem_g_s.at[kind - 1, d], sem_g_r.at[kind - 1, d], x_dev[to])
            one.start()
            sent.append(one)
        to_core(0, d)
        landed(mp.at[d], sem_mp_r.at[d])
        one = remote(mp.at[d], mq.at[d], sem_mq_s.at[d], sem_mq_r.at[d], sibling)
        one.start()
        sent.append(one)
        pltpu.make_async_copy(mp.at[d], smp.at[d], sem_smp.at[d]).start()

    def p_pass(d):
        for kind, to, at_ in ((1, 1, 0), (2, 3, quarter // 2)):
            landed(pg.at[kind, d], sem_g_r.at[kind - 1, d])
            two = pl.ds(at_, quarter // 2)
            one = remote(
                pg.at[kind, d, two], pg.at[3, d, two], sem_g_s.at[1 + kind, d], sem_g_r.at[1 + kind, d], x_dev[to]
            )
            one.start()
            sent.append(one)
        for kind in (1, 2):
            to_core(kind, d)

    def p_done(d):
        for kind, at_ in ((1, 0), (2, quarter // 2)):
            landed(pg.at[3, d, pl.ds(at_, quarter // 2)], sem_g_r.at[1 + kind, d])
        to_core(3, d)

    quarters = [turn(x - z + RING, k) * quarter for k in (0, 3, 1, 2)]

    def p_slab(d):
        landed(mq.at[d], sem_mq_r.at[d])
        two = pltpu.make_async_copy(mq.at[d], smq.at[d], sem_smq.at[d])
        two.start()
        for which, (src, table, base) in enumerate(((pg, smp, core * N_R), (sg, smq, (1 - core) * N_R))):
            for kind in range(4):
                if which:
                    landed(sg.at[kind, d], sem_q_r.at[kind, d])

                def move(s, carry):
                    stage[which, quarters[kind] + s] = src[kind, d, s]
                    return carry

                lax.fori_loop(0, quarter, move, 0, unroll=True)
            if which == 0:
                pltpu.make_async_copy(mp.at[d], smp.at[d], sem_smp.at[d]).wait()
            else:
                two.wait()

            def place(r, carry):
                slab[d, base + r] = jnp.concatenate(
                    [stage[which, table[d, 0, 2 * r]], stage[which, table[d, 0, 2 * r + 1]]], axis=1
                )
                return carry

            lax.fori_loop(0, N_R, place, 0, unroll=4)

    width = a0.shape[-1]
    inner = [turn(y, k) * (2 * N_R // RING) for k in (0, 3, 1, 2)]

    def part(r, d, h):
        cols = slice(None) if h is None else pl.ds(h * width, width)
        left, right = [], []
        for k in range(4):
            for e in range(2):
                left.append(everyone[k][sma[k, 0, 2 * r + e]])
                right.append(slab[d, inner[k] + sma[k, 1, 2 * r + e], :, cols])
        return jnp.dot(
            jnp.concatenate(left, axis=1), jnp.concatenate(right, axis=0), preferred_element_type=jnp.float32
        )

    def put(ref, i, h, value):
        if h is None:
            ref[2 * i] = value[:, :width].astype(ref.dtype)
            ref[2 * i + 1] = value[:, width:].astype(ref.dtype)
        else:
            ref[i] = value.astype(ref.dtype)

    def get(ref, i, h):
        if h is None:
            return jnp.concatenate([ref[2 * i], ref[2 * i + 1]], axis=1).astype(jnp.float32)
        return ref[i].astype(jnp.float32)

    def first(u):
        at_, rows, h = UNITS[u]

        def body(i, carry):
            put(s1.at[u], i, h, part(at_ + i, 2, h))
            return carry

        lax.fori_loop(0, rows, body, 0, unroll=2)
        for kind, to in ((0, 1), (1, 3)):
            one = remote(
                s1.at[u, pl.ds(kind * (PARTS // 2), PARTS // 2)], r1.at[u, kind], sem_1_s.at[u, kind], sem_1_r.at[u, kind], z_dev[to]
            )
            one.start()
            sent.append(one)

    def second(u, kind):
        at_, rows, h = UNITS[u]
        to = (1, 3)[kind]
        lo = kind * (rows // 2)
        other = rows // 2 - lo

        def plain(i, carry):
            put(s2.at[u, kind], i, h, part(at_ + i, to, h))
            return carry

        def added(i, carry):
            put(s2.at[u, kind], lo + i, h, part(at_ + lo + i, to, h) + get(r1.at[u, kind], i, h))
            return carry

        lax.fori_loop(other, other + rows // 2, plain, 0, unroll=2)
        landed(r1.at[u, kind], sem_1_r.at[u, kind])
        lax.fori_loop(0, rows // 2, added, 0, unroll=2)
        one = remote(s2.at[u, kind], r2.at[u, kind], sem_2_s.at[u, kind], sem_2_r.at[u, kind], z_dev[to])
        one.start()
        sent.append(one)

    outs = []

    def third(u):
        at_, rows, h = UNITS[u]
        for kind in range(2):
            landed(r2.at[u, kind], sem_2_r.at[u, kind])

        def body(i, carry):
            total = part(at_ + i, 0, h) + get(r2.at[u, 0], i, h) + get(r2.at[u, 1], i, h)
            if h is None:
                prod[0, at_ + i] = total[:, :width].astype(prod.dtype)
                prod[1, at_ + i] = total[:, width:].astype(prod.dtype)
            else:
                prod[h, at_ + i] = total.astype(prod.dtype)
            return carry

        lax.fori_loop(0, rows, body, 0, unroll=2)
        for k in (0, 1) if h is None else (h,):
            one = pltpu.make_async_copy(
                prod.at[k, pl.ds(at_, rows)],
                prod_out.at[pl.ds(at_, rows), :, pl.ds(k * width, width)],
                sem_out.at[u, k],
            )
            one.start()
            outs.append(one)

    def coarse(c, h):
        t0, t1 = loc[1, 2 * c], loc[1, 2 * c + 1]
        u0, u1 = loc[2, 2 * c], loc[2, 2 * c + 1]
        return jnp.dot(
            jnp.concatenate([r_in[u0], r_in[u1]], axis=1),
            jnp.concatenate([prod[h, t0], prod[h, t1]], axis=0),
            preferred_element_type=jnp.float32,
        )

    order = (2, 1, 3, 0)

    def coarse_core(h):
        for s in order:
            base = turn(x, s) * 8 + (1 - core) * 4

            def body(u, carry):
                cs[h, s, u] = coarse(base + u, h).astype(cs.dtype)
                return carry

            lax.fori_loop(0, 4, body, 0, unroll=2)
            one = remote(cs.at[h, s], cr.at[h, s], sem_c_s.at[h, s], sem_c_r.at[h, s], sibling)
            one.start()
            sent.append(one)

    def coarse_x(h):
        for s in order:
            base = turn(x, s) * 8 + core * 4
            landed(cr.at[h, s], sem_c_r.at[h, s])

            def body(u, carry):
                total = coarse(base + u, h) + cr[h, s, u].astype(jnp.float32)
                if s == 0:
                    coarse_out[u, :, h * width : (h + 1) * width] = total
                else:
                    xs[h, s - 1, u] = total.astype(xs.dtype)
                return carry

            lax.fori_loop(0, 4, body, 0, unroll=2)
            if s > 0:
                one = remote(
                    xs.at[h, s - 1], xr.at[h, s - 1], sem_x_s.at[h, s - 1], sem_x_r.at[h, s - 1], x_dev[s]
                )
                one.start()
                sent.append(one)

    def coarse_end(h):
        for s in (1, 3, 2):
            landed(xr.at[h, s - 1], sem_x_r.at[h, s - 1])
        cols = slice(h * width, (h + 1) * width)

        def body(u, carry):
            total = coarse_out[u, :, cols]
            for s in range(3):
                total = total + xr[h, s, u].astype(jnp.float32)
            coarse_out[u, :, cols] = total
            return carry

        lax.fori_loop(0, 4, body, 0, unroll=True)

    for c in range(2):
        send_own(c)
    lax.fori_loop(3 * TILES, N_A, sort, 0, unroll=4)
    r_load.wait()
    have = -1

    def begin(q):
        nonlocal have
        while have < NEED[q]:
            have += 1
            take_in(have)
        first(q)

    p_start(2)
    p_start(1)
    p_pass(2)
    p_start(3)
    p_start(0)
    pass_on(0)
    p_pass(1)
    p_done(2)
    for k in range(3):
        landed(ma.at[k], sem_ma_r.at[k])
        pltpu.make_async_copy(ma.at[k], sma.at[k + 1], sem_sma.at[k + 1]).start()
    p_pass(3)
    p_done(1)
    pltpu.make_async_copy(meta_a, sma.at[0], sem_sma.at[0]).wait()
    for k in range(3):
        pltpu.make_async_copy(ma.at[k], sma.at[k + 1], sem_sma.at[k + 1]).wait()
    p_slab(2)
    begin(0)
    pass_on(1)
    p_slab(1)
    p_done(3)
    second(0, 0)
    begin(1)
    p_slab(3)
    second(0, 1)
    p_pass(0)
    pass_on(2)
    second(1, 0)
    second(1, 1)
    p_done(0)
    begin(2)
    pass_on(3)
    p_slab(0)
    third(0)
    for q in range(3, STEPS + 2):
        if q < STEPS:
            begin(q)
        if q <= STEPS:
            second(q - 1, 0)
            second(q - 1, 1)
        if q + 1 < CHUNKS:
            pass_on(q + 1)
        third(q - 2)
        if q == STEPS - 1:
            coarse_core(0)
        if q == STEPS:
            coarse_x(0)
    coarse_core(1)
    coarse_end(0)
    coarse_x(1)
    coarse_end(1)

    for one in sent + ma_copies:
        one.wait_send()
    for k in (1, 2, 3):
        for one in p_copy(k):
            one.wait_send()

    @pl.when(jnp.logical_not(keeps))
    def _():
        for one in p_copy(0):
            one.wait_send()

    for one in outs:
        one.wait()


def deliver(product, coarse, product_out, coarse_out, product_here, coarse_here, sems):
    pieces = 8
    rows = product.shape[0] // pieces
    parts = [(product, product_here, product_out, pl.ds(k * rows, rows)) for k in range(pieces)]
    parts.append((coarse, coarse_here, coarse_out, pl.ds(0, coarse.shape[0])))
    loads = [pltpu.make_async_copy(a.at[p], b.at[p], sems.at[0, k]) for k, (a, b, _, p) in enumerate(parts)]
    stores = [pltpu.make_async_copy(b.at[p], c.at[p], sems.at[1, k]) for k, (_, b, c, p) in enumerate(parts)]
    for one in loads:
        one.start()
    for load, store in zip(loads, stores):
        load.wait()
        store.start()
    for one in stores:
        one.wait()


def tables(a_rows, a_cols, p_pos, aggregate, loc, meta_a, meta_p):
    shape = (128, 128)
    down = lax.broadcasted_iota(jnp.int32, shape, 0).astype(jnp.float32)
    along = lax.broadcasted_iota(jnp.int32, shape, 1).astype(jnp.float32)
    far = 1000.0

    def lanes(v):
        v = jnp.concatenate([v.astype(jnp.float32), jnp.full((1, 128 - v.shape[1]), far, jnp.float32)], axis=1)
        return jnp.broadcast_to(v, shape)

    def count(hit, axis):
        return jnp.sum(jnp.where(hit, 1.0, 0.0), axis=axis, keepdims=True)

    def spread(index, value, fill):
        return fill + jnp.sum(jnp.where(index == along, value - fill, 0.0), axis=0, keepdims=True)

    here = lanes(a_rows[...])
    there = here.T
    same = (here == there) & (along < down)
    rank = count((here < there) | same, 1)
    slot = there * 2.0 + count(same, 1)
    perm = spread(rank, down, 0.0)
    pos = spread(slot, rank, float(N_A))
    inner = spread(slot, lanes(a_cols[...]).T, 0.0)
    stored = spread(lanes(p_pos[...]).T, down, float(N_P))
    named = lanes(aggregate[...]).T
    fine = spread(named * 2.0 + count((named == named.T) & (along < down), 1), down, float(N_R))
    none = jnp.zeros((1, 128), jnp.float32)

    def pack(*lines):
        return jnp.concatenate(list(lines) + [none] * (8 - len(lines)), axis=0).astype(jnp.int32)

    loc[...] = pack(perm, fine, jnp.minimum(fine, N_R - 1.0))
    meta_a[...] = pack(pos, inner)
    meta_p[...] = pack(stored)


def local(a_tiles, a_rows, a_cols, p_tiles, p_pos, r_tiles, aggregate):
    b = a_tiles.shape[-1]
    band = 2 * b
    loc, meta_a, meta_p = pl.pallas_call(
        tables, out_shape=(jax.ShapeDtypeStruct((8, 128), jnp.int32),) * 3
    )(a_rows, a_cols, p_pos.T, aggregate.T)
    bf, f32, i32 = jnp.bfloat16, jnp.float32, jnp.int32
    vmem, smem, dma = pltpu.VMEM, pltpu.SMEM, pltpu.SemaphoreType.DMA
    scratch = (
        [vmem((N_A, b, b), bf), vmem((N_R, b, b), bf)]
        + [vmem((N_A + 1, b, b), bf)] * 4
        + [
            vmem((3, N_A, b, b), bf),
            vmem((4, 4, N_P // RING, b, b), bf),
            vmem((4, 4, N_P // RING, b, b), bf),
            vmem((2, N_P + 1, b, b), bf),
            vmem((4, 2 * N_R, b, band), bf),
            vmem((STEPS, PARTS, b, b), bf),
            vmem((STEPS, 2, PARTS // 2, b, b), bf),
            vmem((STEPS, 2, PARTS, b, b), bf),
            vmem((STEPS, 2, PARTS, b, b), bf),
            vmem((2, N_R + 1, b, b), bf),
            vmem((2, 4, 4, b, b), bf),
            vmem((2, 4, 4, b, b), bf),
            vmem((2, 3, 4, b, b), bf),
            vmem((2, 3, 4, b, b), bf),
            vmem((3, 8, 128), i32),
            vmem((4, 8, 128), i32),
            vmem((4, 8, 128), i32),
            smem((4, 8, 128), i32),
            smem((4, 8, 128), i32),
            smem((4, 8, 128), i32),
        ]
        + [dma((4, CHUNKS)), dma((4, CHUNKS))]
        + [dma((4,))] * 2
        + [dma((4, 4))] * 4
        + [dma((3,))] * 2
        + [dma((4,))] * 4
        + [dma((STEPS, 2))] * 4
        + [dma((2, 4))] * 2
        + [dma((2, 3))] * 2
        + [dma((4,)), dma((4,)), dma((4,)), dma((STEPS, 2)), dma((2,))]
    )
    in_vmem = pl.BlockSpec(memory_space=pltpu.VMEM)
    anywhere = pl.BlockSpec(memory_space=pl.ANY)
    product, coarse = pl.pallas_call(
        kernel,
        out_shape=(
            jax.ShapeDtypeStruct((N_R, b, band), bf),
            jax.ShapeDtypeStruct((4, b, band), f32),
        ),
        in_specs=[pl.BlockSpec(memory_space=pltpu.SMEM), in_vmem, in_vmem, anywhere, anywhere, anywhere],
        out_specs=(anywhere, in_vmem),
        scratch_shapes=scratch,
        compiler_params=pltpu.CompilerParams(
            collective_id=0, has_side_effects=True, vmem_limit_bytes=60 * 1024 * 1024
        ),
        cost_estimate=pl.CostEstimate(flops=9 * 10**9, bytes_accessed=10**7, transcendentals=0),
    )(loc, meta_a, meta_p, a_tiles[0], p_tiles[:, 0], r_tiles)
    product, coarse = pl.pallas_call(
        deliver,
        out_shape=(jax.ShapeDtypeStruct(product.shape, bf), jax.ShapeDtypeStruct(coarse.shape, f32)),
        in_specs=[anywhere, anywhere],
        out_specs=(anywhere, anywhere),
        scratch_shapes=[vmem(product.shape, bf), vmem(coarse.shape, f32), dma((2, 9))],
    )(product, coarse)
    return product.reshape(N_R * b, band), coarse.reshape(4 * b, band)


def solution(mesh):
    in_specs = (
        P("row", "col", None, None),
        P("row", "col"),
        P("row", "col"),
        P("row", "col", None, None),
        P("row", "col"),
        P("row", None, None),
        P("row", None),
    )
    out_specs = (P("row", "col"), P("row", "col"))
    return jax.shard_map(local, mesh=mesh, in_specs=in_specs, out_specs=out_specs, check_vma=False)
```

```python
import jax
import jax.numpy as jnp
from jax import lax
from jax.experimental import pallas as pl
from jax.experimental.pallas import tpu as pltpu
from jax.sharding import PartitionSpec as P

MESH = pl.DeviceIdType.MESH

N_A = 48
N_P = 16
N_R = 32
RING = 4
TILES = 8
CHUNKS = N_A // TILES
UNITS = [(0, 4, None), (4, 4, None), (8, 4, None), (12, 4, None), (16, 8, 0), (24, 8, 0), (16, 8, 1), (24, 8, 1)]
STEPS = len(UNITS)
PARTS = 8
NEED = [(min(2 * (r + n), r + n + N_A - N_R) - 1) // TILES for r, n, _ in UNITS]


def kernel(
    a_rows, a_cols, p_pos, aggregate, a_hbm, p_in, r_hbm,
    prod_out, coarse_out,
    loc_here, loc, meta_a, meta_p, a_in, r_in, a0, a1, a2, a3, land_a, pg, sg, stage, slab,
    s1, r1, s2, r2, prod, cs, cr, xs, xr,
    ma, mp, mq, sma, smp, smq,
    sem_a_s, sem_a_r, sem_p_s, sem_p_r, sem_g_s, sem_g_r, sem_q_s, sem_q_r,
    sem_ma_s, sem_ma_r, sem_mp_s, sem_mp_r, sem_mq_s, sem_mq_r,
    sem_1_s, sem_1_r, sem_2_s, sem_2_r,
    sem_c_s, sem_c_r, sem_x_s, sem_x_r,
    sem_sma, sem_smp, sem_smq, sem_out, sem_in, sem_loc,
):
    row, col = lax.axis_index("row"), lax.axis_index("col")
    x, core = lax.div(row, 2), lax.rem(row, 2)
    z, y = lax.div(col, RING), lax.rem(col, RING)

    def at(x_, core_, z_, y_):
        return (x_ * 2 + core_, z_ * RING + y_)

    def turn(v, by):
        return lax.rem(v + by, RING)

    y_dev = [at(x, core, z, turn(y, k)) for k in range(RING)]
    z_dev = [at(x, core, turn(z, k), y) for k in range(RING)]
    x_dev = [at(turn(x, k), core, z, y) for k in range(RING)]
    p_to = [at(turn(x, k), core, x, y) for k in range(RING)]
    p_from = [at(z, core, turn(z, k), y) for k in range(RING)]
    sibling = at(x, 1 - core, z, y)
    keeps = x == z

    a_load = pltpu.make_async_copy(a_hbm, a_in, sem_in.at[0])
    r_load = pltpu.make_async_copy(r_hbm, r_in, sem_in.at[1])
    a_load.start()
    r_load.start()

    def remote(src, dst, send, recv, to):
        return pltpu.make_async_remote_copy(
            src_ref=src, dst_ref=dst, send_sem=send, recv_sem=recv, device_id=to, device_id_type=MESH
        )

    def landed(ref, sem):
        pltpu.make_async_copy(ref, ref, sem).wait()

    barrier = pltpu.get_barrier_semaphore()

    def greet(to):
        pl.semaphore_signal(barrier, inc=1, device_id=to, device_id_type=MESH)

    for to in y_dev[1:] + [z_dev[1], z_dev[3]] + x_dev[1:] + [sibling] + p_to[1:] + p_from[1:]:
        greet(to)

    @pl.when(jnp.logical_not(keeps))
    def _():
        greet(p_to[0])
        greet(p_from[0])

    for one in (loc_here, meta_a, meta_p):
        one[...] = jnp.zeros(one.shape, one.dtype)
    tables(a_rows, a_cols, p_pos, aggregate, loc_here, meta_a, meta_p)
    loc_copy = pltpu.make_async_copy(loc_here, loc, sem_loc)
    loc_copy.start()
    pltpu.make_async_copy(meta_a, sma.at[0], sem_sma.at[0]).start()
    everyone = (a0, a1, a2, a3)
    zero = jnp.zeros(a0.shape[1:], a0.dtype)
    for one in everyone:
        one[N_A] = zero
    stage[0, N_P] = zero
    stage[1, N_P] = zero
    prod[0, N_R] = zero
    prod[1, N_R] = zero
    a_load.wait()
    loc_copy.wait()

    def sort(s, carry):
        a0[s] = a_in[loc[0, s]]
        return carry

    lax.fori_loop(0, 3 * TILES, sort, 0, unroll=4)
    pl.semaphore_wait(barrier, jnp.where(keeps, 15, 17))

    quarter = N_P // RING

    def p_copy(k):
        d = turn(z - x + RING, 0)
        return (
            remote(p_in.at[pl.ds(k * quarter, quarter)], pg.at[0, d], sem_p_s.at[k], sem_p_r.at[d], p_to[k]),
            remote(meta_p, mp.at[d], sem_mp_s.at[k], sem_mp_r.at[d], p_to[k]),
        )

    for k in (1, 2, 3):
        for one in p_copy(k):
            one.start()

    @pl.when(jnp.logical_not(keeps))
    def _():
        for one in p_copy(0):
            one.start()

    @pl.when(keeps)
    def _():
        pltpu.make_async_copy(p_in.at[pl.ds(0, quarter)], pg.at[0, 0], sem_p_r.at[0]).start()
        pltpu.make_async_copy(meta_p, mp.at[0], sem_mp_r.at[0]).start()

    ma_copies = [
        remote(meta_a, ma.at[k], sem_ma_s.at[k], sem_ma_r.at[k], y_dev[to])
        for k, to in ((0, 1), (1, 3), (2, 2))
    ]
    for one in ma_copies:
        one.start()
    sent = []

    def send_own(c):
        part = pl.ds(c * TILES, TILES)
        for kind, to in ((0, 1), (1, 3)):
            one = remote(a0.at[part], land_a.at[kind, part], sem_a_s.at[kind, c], sem_a_r.at[kind, c], y_dev[to])
            one.start()
            sent.append(one)

    half = TILES // 2

    def pass_on(c):
        whole = pl.ds(c * TILES, TILES)
        for kind, to, at_ in ((0, 1, c * TILES), (1, 3, c * TILES + half)):
            landed(land_a.at[kind, whole], sem_a_r.at[kind, c])
            part = pl.ds(at_, half)
            one = remote(
                land_a.at[kind, part], land_a.at[2, part], sem_a_s.at[2 + kind, c], sem_a_r.at[2 + kind, c], y_dev[to]
            )
            one.start()
            sent.append(one)
        if c + 2 < CHUNKS:
            send_own(c + 2)

    def take_in(c):
        for kind, at_ in ((0, c * TILES), (1, c * TILES + half)):
            landed(land_a.at[2, pl.ds(at_, half)], sem_a_r.at[2 + kind, c])

        def move(s, carry):
            a1[s] = land_a[0, s]
            a2[s] = land_a[1, s]
            a3[s] = land_a[2, s]
            return carry

        lax.fori_loop(c * TILES, (c + 1) * TILES, move, 0, unroll=2)

    def to_core(kind, d):
        one = remote(pg.at[kind, d], sg.at[kind, d], sem_q_s.at[kind, d], sem_q_r.at[kind, d], sibling)
        one.start()
        sent.append(one)

    def p_start(d):
        landed(pg.at[0, d], sem_p_r.at[d])
        for kind, to in ((1, 1), (2, 3)):
            one = remote(pg.at[0, d], pg.at[kind, d], sem_g_s.at[kind - 1, d], sem_g_r.at[kind - 1, d], x_dev[to])
            one.start()
            sent.append(one)
        to_core(0, d)
        landed(mp.at[d], sem_mp_r.at[d])
        one = remote(mp.at[d], mq.at[d], sem_mq_s.at[d], sem_mq_r.at[d], sibling)
        one.start()
        sent.append(one)
        pltpu.make_async_copy(mp.at[d], smp.at[d], sem_smp.at[d]).start()

    def p_pass(d):
        for kind, to, at_ in ((1, 1, 0), (2, 3, quarter // 2)):
            landed(pg.at[kind, d], sem_g_r.at[kind - 1, d])
            two = pl.ds(at_, quarter // 2)
            one = remote(
                pg.at[kind, d, two], pg.at[3, d, two], sem_g_s.at[1 + kind, d], sem_g_r.at[1 + kind, d], x_dev[to]
            )
            one.start()
            sent.append(one)
        for kind in (1, 2):
            to_core(kind, d)

    def p_done(d):
        for kind, at_ in ((1, 0), (2, quarter // 2)):
            landed(pg.at[3, d, pl.ds(at_, quarter // 2)], sem_g_r.at[1 + kind, d])
        to_core(3, d)

    quarters = [turn(x - z + RING, k) * quarter for k in (0, 3, 1, 2)]

    def p_slab(d):
        landed(mq.at[d], sem_mq_r.at[d])
        two = pltpu.make_async_copy(mq.at[d], smq.at[d], sem_smq.at[d])
        two.start()
        for which, (src, table, base) in enumerate(((pg, smp, core * N_R), (sg, smq, (1 - core) * N_R))):
            for kind in range(4):
                if which:
                    landed(sg.at[kind, d], sem_q_r.at[kind, d])

                def move(s, carry):
                    stage[which, quarters[kind] + s] = src[kind, d, s]
                    return carry

                lax.fori_loop(0, quarter, move, 0, unroll=True)
            if which == 0:
                pltpu.make_async_copy(mp.at[d], smp.at[d], sem_smp.at[d]).wait()
            else:
                two.wait()

            def place(r, carry):
                slab[d, base + r] = jnp.concatenate(
                    [stage[which, table[d, 0, 2 * r]], stage[which, table[d, 0, 2 * r + 1]]], axis=1
                )
                return carry

            lax.fori_loop(0, N_R, place, 0, unroll=4)

    width = a0.shape[-1]
    inner = [turn(y, k) * (2 * N_R // RING) for k in (0, 3, 1, 2)]

    def part(r, d, h):
        cols = slice(None) if h is None else pl.ds(h * width, width)
        left, right = [], []
        for k in range(4):
            for e in range(2):
                left.append(everyone[k][sma[k, 0, 2 * r + e]])
                right.append(slab[d, inner[k] + sma[k, 1, 2 * r + e], :, cols])
        return jnp.dot(
            jnp.concatenate(left, axis=1), jnp.concatenate(right, axis=0), preferred_element_type=jnp.float32
        )

    def put(ref, i, h, value):
        if h is None:
            ref[2 * i] = value[:, :width].astype(ref.dtype)
            ref[2 * i + 1] = value[:, width:].astype(ref.dtype)
        else:
            ref[i] = value.astype(ref.dtype)

    def get(ref, i, h):
        if h is None:
            return jnp.concatenate([ref[2 * i], ref[2 * i + 1]], axis=1).astype(jnp.float32)
        return ref[i].astype(jnp.float32)

    def first(u):
        at_, rows, h = UNITS[u]

        def body(i, carry):
            put(s1.at[u], i, h, part(at_ + i, 2, h))
            return carry

        lax.fori_loop(0, rows, body, 0, unroll=2)
        for kind, to in ((0, 1), (1, 3)):
            one = remote(
                s1.at[u, pl.ds(kind * (PARTS // 2), PARTS // 2)], r1.at[u, kind], sem_1_s.at[u, kind], sem_1_r.at[u, kind], z_dev[to]
            )
            one.start()
            sent.append(one)

    def second(u, kind):
        at_, rows, h = UNITS[u]
        to = (1, 3)[kind]
        lo = kind * (rows // 2)
        other = rows // 2 - lo

        def plain(i, carry):
            put(s2.at[u, kind], i, h, part(at_ + i, to, h))
            return carry

        def added(i, carry):
            put(s2.at[u, kind], lo + i, h, part(at_ + lo + i, to, h) + get(r1.at[u, kind], i, h))
            return carry

        lax.fori_loop(other, other + rows // 2, plain, 0, unroll=2)
        landed(r1.at[u, kind], sem_1_r.at[u, kind])
        lax.fori_loop(0, rows // 2, added, 0, unroll=2)
        one = remote(s2.at[u, kind], r2.at[u, kind], sem_2_s.at[u, kind], sem_2_r.at[u, kind], z_dev[to])
        one.start()
        sent.append(one)

    outs = []

    def third(u):
        at_, rows, h = UNITS[u]
        for kind in range(2):
            landed(r2.at[u, kind], sem_2_r.at[u, kind])

        def body(i, carry):
            total = part(at_ + i, 0, h) + get(r2.at[u, 0], i, h) + get(r2.at[u, 1], i, h)
            if h is None:
                prod[0, at_ + i] = total[:, :width].astype(prod.dtype)
                prod[1, at_ + i] = total[:, width:].astype(prod.dtype)
            else:
                prod[h, at_ + i] = total.astype(prod.dtype)
            return carry

        lax.fori_loop(0, rows, body, 0, unroll=2)
        for k in (0, 1) if h is None else (h,):
            one = pltpu.make_async_copy(
                prod.at[k, pl.ds(at_, rows)],
                prod_out.at[pl.ds(at_, rows), :, pl.ds(k * width, width)],
                sem_out.at[u, k],
            )
            one.start()
            outs.append(one)

    def coarse(c, h):
        t0, t1 = loc[1, 2 * c], loc[1, 2 * c + 1]
        u0, u1 = loc[2, 2 * c], loc[2, 2 * c + 1]
        return jnp.dot(
            jnp.concatenate([r_in[u0], r_in[u1]], axis=1),
            jnp.concatenate([prod[h, t0], prod[h, t1]], axis=0),
            preferred_element_type=jnp.float32,
        )

    order = (2, 1, 3, 0)

    def coarse_core(h):
        for s in order:
            base = turn(x, s) * 8 + (1 - core) * 4

            def body(u, carry):
                cs[h, s, u] = coarse(base + u, h).astype(cs.dtype)
                return carry

            lax.fori_loop(0, 4, body, 0, unroll=2)
            one = remote(cs.at[h, s], cr.at[h, s], sem_c_s.at[h, s], sem_c_r.at[h, s], sibling)
            one.start()
            sent.append(one)

    def coarse_x(h):
        for s in order:
            base = turn(x, s) * 8 + core * 4
            landed(cr.at[h, s], sem_c_r.at[h, s])

            def body(u, carry):
                total = coarse(base + u, h) + cr[h, s, u].astype(jnp.float32)
                if s == 0:
                    coarse_out[u, :, h * width : (h + 1) * width] = total
                else:
                    xs[h, s - 1, u] = total.astype(xs.dtype)
                return carry

            lax.fori_loop(0, 4, body, 0, unroll=2)
            if s > 0:
                one = remote(
                    xs.at[h, s - 1], xr.at[h, s - 1], sem_x_s.at[h, s - 1], sem_x_r.at[h, s - 1], x_dev[s]
                )
                one.start()
                sent.append(one)

    def coarse_end(h):
        for s in (1, 3, 2):
            landed(xr.at[h, s - 1], sem_x_r.at[h, s - 1])
        cols = slice(h * width, (h + 1) * width)

        def body(u, carry):
            total = coarse_out[u, :, cols]
            for s in range(3):
                total = total + xr[h, s, u].astype(jnp.float32)
            coarse_out[u, :, cols] = total
            return carry

        lax.fori_loop(0, 4, body, 0, unroll=2)

    for c in range(2):
        send_own(c)
    lax.fori_loop(3 * TILES, N_A, sort, 0, unroll=2)
    r_load.wait()
    have = -1

    def begin(q):
        nonlocal have
        while have < NEED[q]:
            have += 1
            take_in(have)
        first(q)

    p_start(2)
    p_start(1)
    p_pass(2)
    p_start(3)
    p_start(0)
    pass_on(0)
    p_pass(1)
    p_done(2)
    for k in range(3):
        landed(ma.at[k], sem_ma_r.at[k])
        pltpu.make_async_copy(ma.at[k], sma.at[k + 1], sem_sma.at[k + 1]).start()
    p_pass(3)
    p_done(1)
    pltpu.make_async_copy(meta_a, sma.at[0], sem_sma.at[0]).wait()
    for k in range(3):
        pltpu.make_async_copy(ma.at[k], sma.at[k + 1], sem_sma.at[k + 1]).wait()
    p_slab(2)
    begin(0)
    pass_on(1)
    p_slab(1)
    p_done(3)
    second(0, 0)
    begin(1)
    p_slab(3)
    second(0, 1)
    p_pass(0)
    pass_on(2)
    second(1, 0)
    second(1, 1)
    p_done(0)
    begin(2)
    pass_on(3)
    p_slab(0)
    third(0)
    for q in range(3, STEPS + 2):
        if q < STEPS:
            begin(q)
        if q <= STEPS:
            second(q - 1, 0)
            second(q - 1, 1)
        if q + 1 < CHUNKS:
            pass_on(q + 1)
        third(q - 2)
        if q == STEPS - 1:
            coarse_core(0)
        if q == STEPS:
            coarse_x(0)
    coarse_core(1)
    coarse_end(0)
    coarse_x(1)
    coarse_end(1)

    for one in sent + ma_copies:
        one.wait_send()
    for k in (1, 2, 3):
        for one in p_copy(k):
            one.wait_send()

    @pl.when(jnp.logical_not(keeps))
    def _():
        for one in p_copy(0):
            one.wait_send()

    for one in outs:
        one.wait()


def deliver(product, coarse, product_out, coarse_out, product_here, coarse_here, sems):
    pieces = 8
    rows = product.shape[0] // pieces
    parts = [(product, product_here, product_out, pl.ds(k * rows, rows)) for k in range(pieces)]
    parts.append((coarse, coarse_here, coarse_out, pl.ds(0, coarse.shape[0])))
    loads = [pltpu.make_async_copy(a.at[p], b.at[p], sems.at[0, k]) for k, (a, b, _, p) in enumerate(parts)]
    stores = [pltpu.make_async_copy(b.at[p], c.at[p], sems.at[1, k]) for k, (_, b, c, p) in enumerate(parts)]
    for one in loads:
        one.start()
    for load, store in zip(loads, stores):
        load.wait()
        store.start()
    for one in stores:
        one.wait()


def tables(a_rows, a_cols, p_pos, aggregate, loc, meta_a, meta_p):
    shape = (128, 128)
    down = lax.broadcasted_iota(jnp.int32, shape, 0)
    along = lax.broadcasted_iota(jnp.int32, shape, 1)

    def lanes(v):
        v = jnp.concatenate([v, jnp.full((1, 128 - v.shape[1]), 1000, jnp.int32)], axis=1)
        return jnp.broadcast_to(v, shape)

    def count(hit):
        return jnp.broadcast_to(jnp.sum(jnp.where(hit, 1, 0), axis=0, keepdims=True), shape)

    def spread(index, value, fill, most):
        found = fill + jnp.sum(jnp.where(index == along, value - fill, 0), axis=0, keepdims=True)
        return jnp.clip(found, 0, most)

    here = lanes(a_rows[...])
    there = here.T
    same = (there == here) & (down < along)
    rank = count((there < here) | same).T
    slot = (here * 2 + count(same)).T
    loc[0:1] = spread(rank, down, 0, N_A - 1)
    meta_a[0:1] = spread(slot, rank, N_A, N_A)
    meta_a[1:2] = spread(slot, lanes(a_cols[...]).T, 0, 2 * N_R // RING - 1)
    meta_p[0:1] = spread(lanes(p_pos[...]).T, down, N_P, N_P)
    named = lanes(aggregate[...])
    fine = spread((named * 2 + count((named.T == named) & (down < along))).T, down, N_R, N_R)
    loc[1:2] = fine
    loc[2:3] = jnp.minimum(fine, N_R - 1)


def local(a_tiles, a_rows, a_cols, p_tiles, p_pos, r_tiles, aggregate):
    b = a_tiles.shape[-1]
    band = 2 * b
    bf, f32, i32 = jnp.bfloat16, jnp.float32, jnp.int32
    vmem, smem, dma = pltpu.VMEM, pltpu.SMEM, pltpu.SemaphoreType.DMA
    scratch = (
        [vmem((8, 128), i32), smem((8, 128), i32), vmem((8, 128), i32), vmem((8, 128), i32)]
        + [vmem((N_A, b, b), bf), vmem((N_R, b, b), bf)]
        + [vmem((N_A + 1, b, b), bf)] * 4
        + [
            vmem((3, N_A, b, b), bf),
            vmem((4, 4, N_P // RING, b, b), bf),
            vmem((4, 4, N_P // RING, b, b), bf),
            vmem((2, N_P + 1, b, b), bf),
            vmem((4, 2 * N_R, b, band), bf),
            vmem((STEPS, PARTS, b, b), bf),
            vmem((STEPS, 2, PARTS // 2, b, b), bf),
            vmem((STEPS, 2, PARTS, b, b), bf),
            vmem((STEPS, 2, PARTS, b, b), bf),
            vmem((2, N_R + 1, b, b), bf),
            vmem((2, 4, 4, b, b), bf),
            vmem((2, 4, 4, b, b), bf),
            vmem((2, 3, 4, b, b), bf),
            vmem((2, 3, 4, b, b), bf),
            vmem((3, 8, 128), i32),
            vmem((4, 8, 128), i32),
            vmem((4, 8, 128), i32),
            smem((4, 8, 128), i32),
            smem((4, 8, 128), i32),
            smem((4, 8, 128), i32),
        ]
        + [dma((4, CHUNKS)), dma((4, CHUNKS))]
        + [dma((4,))] * 2
        + [dma((4, 4))] * 4
        + [dma((3,))] * 2
        + [dma((4,))] * 4
        + [dma((STEPS, 2))] * 4
        + [dma((2, 4))] * 2
        + [dma((2, 3))] * 2
        + [dma((4,)), dma((4,)), dma((4,)), dma((STEPS, 2)), dma((2,)), dma]
    )
    in_vmem = pl.BlockSpec(memory_space=pltpu.VMEM)
    anywhere = pl.BlockSpec(memory_space=pl.ANY)
    product, coarse = pl.pallas_call(
        kernel,
        out_shape=(
            jax.ShapeDtypeStruct((N_R, b, band), bf),
            jax.ShapeDtypeStruct((4, b, band), f32),
        ),
        in_specs=[in_vmem] * 4 + [anywhere] * 3,
        out_specs=(anywhere, in_vmem),
        scratch_shapes=scratch,
        compiler_params=pltpu.CompilerParams(
            collective_id=0, has_side_effects=True, vmem_limit_bytes=60 * 1024 * 1024
        ),
        cost_estimate=pl.CostEstimate(flops=9 * 10**9, bytes_accessed=10**7, transcendentals=0),
    )(a_rows, a_cols, p_pos.T, aggregate.T, a_tiles[0], p_tiles[:, 0], r_tiles)
    product, coarse = pl.pallas_call(
        deliver,
        out_shape=(jax.ShapeDtypeStruct(product.shape, bf), jax.ShapeDtypeStruct(coarse.shape, f32)),
        in_specs=[anywhere, anywhere],
        out_specs=(anywhere, anywhere),
        scratch_shapes=[vmem(product.shape, bf), vmem(coarse.shape, f32), dma((2, 9))],
    )(product, coarse)
    return product.reshape(N_R * b, band), coarse.reshape(4 * b, band)


def solution(mesh):
    in_specs = (
        P("row", "col", None, None),
        P("row", "col"),
        P("row", "col"),
        P("row", "col", None, None),
        P("row", "col"),
        P("row", None, None),
        P("row", None),
    )
    out_specs = (P("row", "col"), P("row", "col"))
    return jax.shard_map(local, mesh=mesh, in_specs=in_specs, out_specs=out_specs, check_vma=False)
```

```python
import jax
import jax.numpy as jnp
from jax import lax
from jax.experimental import pallas as pl
from jax.experimental.pallas import tpu as pltpu
from jax.sharding import PartitionSpec as P

MESH = pl.DeviceIdType.MESH

N_A = 48
N_P = 16
N_R = 32
RING = 4
TILES = 8
CHUNKS = N_A // TILES
UNITS = [(0, 4, None), (4, 4, None), (8, 4, None), (12, 4, None), (16, 8, 0), (24, 8, 0), (16, 8, 1), (24, 8, 1)]
STEPS = len(UNITS)
PARTS = 8
NEED = [(min(2 * (r + n), r + n + N_A - N_R) - 1) // TILES for r, n, _ in UNITS]


def kernel(
    a_rows, a_cols, p_pos, aggregate, a_hbm, p_in, r_hbm,
    prod_out, coarse_out,
    loc_here, loc, meta_a, meta_p, a_in, r_in, a0, a1, a2, a3, land_a, pg, sg, stage, slab,
    s1, r1, s2, r2, prod, cs, cr, xs, xr,
    ma, mp, mq, sma, smp, smq,
    sem_a_s, sem_a_r, sem_p_s, sem_p_r, sem_g_s, sem_g_r, sem_q_s, sem_q_r,
    sem_ma_s, sem_ma_r, sem_mp_s, sem_mp_r, sem_mq_s, sem_mq_r,
    sem_1_s, sem_1_r, sem_2_s, sem_2_r,
    sem_c_s, sem_c_r, sem_x_s, sem_x_r,
    sem_sma, sem_smp, sem_smq, sem_out, sem_in, sem_loc,
):
    row, col = lax.axis_index("row"), lax.axis_index("col")
    x, core = lax.div(row, 2), lax.rem(row, 2)
    z, y = lax.div(col, RING), lax.rem(col, RING)

    def at(x_, core_, z_, y_):
        return (x_ * 2 + core_, z_ * RING + y_)

    def turn(v, by):
        return lax.rem(v + by, RING)

    y_dev = [at(x, core, z, turn(y, k)) for k in range(RING)]
    z_dev = [at(x, core, turn(z, k), y) for k in range(RING)]
    x_dev = [at(turn(x, k), core, z, y) for k in range(RING)]
    p_to = [at(turn(x, k), core, x, y) for k in range(RING)]
    p_from = [at(z, core, turn(z, k), y) for k in range(RING)]
    sibling = at(x, 1 - core, z, y)
    keeps = x == z

    a_load = pltpu.make_async_copy(a_hbm, a_in, sem_in.at[0])
    r_load = pltpu.make_async_copy(r_hbm, r_in, sem_in.at[1])
    a_load.start()
    r_load.start()

    def remote(src, dst, send, recv, to):
        return pltpu.make_async_remote_copy(
            src_ref=src, dst_ref=dst, send_sem=send, recv_sem=recv, device_id=to, device_id_type=MESH
        )

    def landed(ref, sem):
        pltpu.make_async_copy(ref, ref, sem).wait()

    barrier = pltpu.get_barrier_semaphore()

    def greet(to):
        pl.semaphore_signal(barrier, inc=1, device_id=to, device_id_type=MESH)

    for to in y_dev[1:] + [z_dev[1], z_dev[3]] + x_dev[1:] + [sibling] + p_to[1:] + p_from[1:]:
        greet(to)

    @pl.when(jnp.logical_not(keeps))
    def _():
        greet(p_to[0])
        greet(p_from[0])

    for one in (loc_here, meta_a, meta_p):
        one[...] = jnp.zeros(one.shape, one.dtype)
    tables(a_rows, a_cols, p_pos, aggregate, loc_here, meta_a, meta_p)
    loc_copy = pltpu.make_async_copy(loc_here, loc, sem_loc)
    loc_copy.start()
    pltpu.make_async_copy(meta_a, sma.at[0], sem_sma.at[0]).start()
    everyone = (a0, a1, a2, a3)
    zero = jnp.zeros(a0.shape[1:], a0.dtype)
    for one in everyone:
        one[N_A] = zero
    stage[0, N_P] = zero
    stage[1, N_P] = zero
    prod[0, N_R] = zero
    prod[1, N_R] = zero
    a_load.wait()
    loc_copy.wait()

    def sort(s, carry):
        a0[s] = a_in[loc[0, s]]
        return carry

    lax.fori_loop(0, 3 * TILES, sort, 0, unroll=4)
    pl.semaphore_wait(barrier, jnp.where(keeps, 15, 17))

    quarter = N_P // RING

    def p_copy(k):
        d = turn(z - x + RING, 0)
        return (
            remote(p_in.at[pl.ds(k * quarter, quarter)], pg.at[0, d], sem_p_s.at[k], sem_p_r.at[d], p_to[k]),
            remote(meta_p, mp.at[d], sem_mp_s.at[k], sem_mp_r.at[d], p_to[k]),
        )

    for k in (1, 2, 3):
        for one in p_copy(k):
            one.start()

    @pl.when(jnp.logical_not(keeps))
    def _():
        for one in p_copy(0):
            one.start()

    @pl.when(keeps)
    def _():
        pltpu.make_async_copy(p_in.at[pl.ds(0, quarter)], pg.at[0, 0], sem_p_r.at[0]).start()
        pltpu.make_async_copy(meta_p, mp.at[0], sem_mp_r.at[0]).start()

    ma_copies = [
        remote(meta_a, ma.at[k], sem_ma_s.at[k], sem_ma_r.at[k], y_dev[to])
        for k, to in ((0, 1), (1, 3), (2, 2))
    ]
    for one in ma_copies:
        one.start()
    sent = []

    def send_own(c):
        part = pl.ds(c * TILES, TILES)
        for kind, to in ((0, 1), (1, 3)):
            one = remote(a0.at[part], land_a.at[kind, part], sem_a_s.at[kind, c], sem_a_r.at[kind, c], y_dev[to])
            one.start()
            sent.append(one)

    half = TILES // 2

    def pass_on(c):
        whole = pl.ds(c * TILES, TILES)
        for kind, to, at_ in ((0, 1, c * TILES), (1, 3, c * TILES + half)):
            landed(land_a.at[kind, whole], sem_a_r.at[kind, c])
            part = pl.ds(at_, half)
            one = remote(
                land_a.at[kind, part], land_a.at[2, part], sem_a_s.at[2 + kind, c], sem_a_r.at[2 + kind, c], y_dev[to]
            )
            one.start()
            sent.append(one)
        if c + 2 < CHUNKS:
            send_own(c + 2)

    def take_in(c):
        for kind, at_ in ((0, c * TILES), (1, c * TILES + half)):
            landed(land_a.at[2, pl.ds(at_, half)], sem_a_r.at[2 + kind, c])

        def move(s, carry):
            a1[s] = land_a[0, s]
            a2[s] = land_a[1, s]
            a3[s] = land_a[2, s]
            return carry

        lax.fori_loop(c * TILES, (c + 1) * TILES, move, 0, unroll=2)

    def to_core(kind, d):
        one = remote(pg.at[kind, d], sg.at[kind, d], sem_q_s.at[kind, d], sem_q_r.at[kind, d], sibling)
        one.start()
        sent.append(one)

    def p_start(d):
        landed(pg.at[0, d], sem_p_r.at[d])
        for kind, to in ((1, 1), (2, 3)):
            one = remote(pg.at[0, d], pg.at[kind, d], sem_g_s.at[kind - 1, d], sem_g_r.at[kind - 1, d], x_dev[to])
            one.start()
            sent.append(one)
        to_core(0, d)
        landed(mp.at[d], sem_mp_r.at[d])
        one = remote(mp.at[d], mq.at[d], sem_mq_s.at[d], sem_mq_r.at[d], sibling)
        one.start()
        sent.append(one)
        pltpu.make_async_copy(mp.at[d], smp.at[d], sem_smp.at[d]).start()

    def p_pass(d):
        for kind, to, at_ in ((1, 1, 0), (2, 3, quarter // 2)):
            landed(pg.at[kind, d], sem_g_r.at[kind - 1, d])
            two = pl.ds(at_, quarter // 2)
            one = remote(
                pg.at[kind, d, two], pg.at[3, d, two], sem_g_s.at[1 + kind, d], sem_g_r.at[1 + kind, d], x_dev[to]
            )
            one.start()
            sent.append(one)
        for kind in (1, 2):
            to_core(kind, d)

    def p_done(d):
        for kind, at_ in ((1, 0), (2, quarter // 2)):
            landed(pg.at[3, d, pl.ds(at_, quarter // 2)], sem_g_r.at[1 + kind, d])
        to_core(3, d)

    quarters = [turn(x - z + RING, k) * quarter for k in (0, 3, 1, 2)]

    def p_slab(d):
        landed(mq.at[d], sem_mq_r.at[d])
        two = pltpu.make_async_copy(mq.at[d], smq.at[d], sem_smq.at[d])
        two.start()
        for which, (src, table, base) in enumerate(((pg, smp, core * N_R), (sg, smq, (1 - core) * N_R))):
            for kind in range(4):
                if which:
                    landed(sg.at[kind, d], sem_q_r.at[kind, d])

                def move(s, carry):
                    stage[which, quarters[kind] + s] = src[kind, d, s]
                    return carry

                lax.fori_loop(0, quarter, move, 0, unroll=True)
            if which == 0:
                pltpu.make_async_copy(mp.at[d], smp.at[d], sem_smp.at[d]).wait()
            else:
                two.wait()

            def place(r, carry):
                slab[d, base + r] = jnp.concatenate(
                    [stage[which, table[d, 0, 2 * r]], stage[which, table[d, 0, 2 * r + 1]]], axis=1
                )
                return carry

            lax.fori_loop(0, N_R, place, 0, unroll=4)

    width = a0.shape[-1]
    inner = [turn(y, k) * (2 * N_R // RING) for k in (0, 3, 1, 2)]

    def part(r, d, h):
        cols = slice(None) if h is None else pl.ds(h * width, width)
        left, right = [], []
        for k in range(4):
            for e in range(2):
                left.append(everyone[k][sma[k, 0, 2 * r + e]])
                right.append(slab[d, inner[k] + sma[k, 1, 2 * r + e], :, cols])
        return jnp.dot(
            jnp.concatenate(left, axis=1), jnp.concatenate(right, axis=0), preferred_element_type=jnp.float32
        )

    def put(ref, i, h, value):
        if h is None:
            ref[2 * i] = value[:, :width].astype(ref.dtype)
            ref[2 * i + 1] = value[:, width:].astype(ref.dtype)
        else:
            ref[i] = value.astype(ref.dtype)

    def get(ref, i, h):
        if h is None:
            return jnp.concatenate([ref[2 * i], ref[2 * i + 1]], axis=1).astype(jnp.float32)
        return ref[i].astype(jnp.float32)

    def first(u):
        at_, rows, h = UNITS[u]

        def body(i, carry):
            put(s1.at[u], i, h, part(at_ + i, 2, h))
            return carry

        lax.fori_loop(0, rows, body, 0, unroll=2)
        for kind, to in ((0, 1), (1, 3)):
            one = remote(
                s1.at[u, pl.ds(kind * (PARTS // 2), PARTS // 2)], r1.at[u, kind], sem_1_s.at[u, kind], sem_1_r.at[u, kind], z_dev[to]
            )
            one.start()
            sent.append(one)

    def second(u, kind):
        at_, rows, h = UNITS[u]
        to = (1, 3)[kind]
        lo = kind * (rows // 2)
        other = rows // 2 - lo

        def plain(i, carry):
            put(s2.at[u, kind], i, h, part(at_ + i, to, h))
            return carry

        def added(i, carry):
            put(s2.at[u, kind], lo + i, h, part(at_ + lo + i, to, h) + get(r1.at[u, kind], i, h))
            return carry

        lax.fori_loop(other, other + rows // 2, plain, 0, unroll=2)
        landed(r1.at[u, kind], sem_1_r.at[u, kind])
        lax.fori_loop(0, rows // 2, added, 0, unroll=2)
        one = remote(s2.at[u, kind], r2.at[u, kind], sem_2_s.at[u, kind], sem_2_r.at[u, kind], z_dev[to])
        one.start()
        sent.append(one)

    outs = []

    def third(u):
        at_, rows, h = UNITS[u]
        for kind in range(2):
            landed(r2.at[u, kind], sem_2_r.at[u, kind])

        def body(i, carry):
            total = part(at_ + i, 0, h) + get(r2.at[u, 0], i, h) + get(r2.at[u, 1], i, h)
            if h is None:
                prod[0, at_ + i] = total[:, :width].astype(prod.dtype)
                prod[1, at_ + i] = total[:, width:].astype(prod.dtype)
            else:
                prod[h, at_ + i] = total.astype(prod.dtype)
            return carry

        lax.fori_loop(0, rows, body, 0, unroll=2)
        for k in (0, 1) if h is None else (h,):
            one = pltpu.make_async_copy(
                prod.at[k, pl.ds(at_, rows)],
                prod_out.at[pl.ds(at_, rows), :, pl.ds(k * width, width)],
                sem_out.at[u, k],
            )
            one.start()
            outs.append(one)

    def coarse(c, h):
        t0, t1 = loc[1, 2 * c], loc[1, 2 * c + 1]
        u0, u1 = loc[2, 2 * c], loc[2, 2 * c + 1]
        return jnp.dot(
            jnp.concatenate([r_in[u0], r_in[u1]], axis=1),
            jnp.concatenate([prod[h, t0], prod[h, t1]], axis=0),
            preferred_element_type=jnp.float32,
        )

    order = (2, 1, 3, 0)

    def coarse_core(h, which=order):
        for s in which:
            base = turn(x, s) * 8 + (1 - core) * 4

            def body(u, carry):
                cs[h, s, u] = coarse(base + u, h).astype(cs.dtype)
                return carry

            lax.fori_loop(0, 4, body, 0, unroll=2)
            one = remote(cs.at[h, s], cr.at[h, s], sem_c_s.at[h, s], sem_c_r.at[h, s], sibling)
            one.start()
            sent.append(one)

    def coarse_x(h, which=order):
        for s in which:
            base = turn(x, s) * 8 + core * 4
            landed(cr.at[h, s], sem_c_r.at[h, s])

            def body(u, carry):
                total = coarse(base + u, h) + cr[h, s, u].astype(jnp.float32)
                if s == 0:
                    coarse_out[u, :, h * width : (h + 1) * width] = total
                else:
                    xs[h, s - 1, u] = total.astype(xs.dtype)
                return carry

            lax.fori_loop(0, 4, body, 0, unroll=2)
            if s > 0:
                one = remote(
                    xs.at[h, s - 1], xr.at[h, s - 1], sem_x_s.at[h, s - 1], sem_x_r.at[h, s - 1], x_dev[s]
                )
                one.start()
                sent.append(one)

    def coarse_end(h):
        for s in (1, 3, 2):
            landed(xr.at[h, s - 1], sem_x_r.at[h, s - 1])
        cols = slice(h * width, (h + 1) * width)

        def body(u, carry):
            total = coarse_out[u, :, cols]
            for s in range(3):
                total = total + xr[h, s, u].astype(jnp.float32)
            coarse_out[u, :, cols] = total
            return carry

        lax.fori_loop(0, 4, body, 0, unroll=2)

    for c in range(2):
        send_own(c)
    lax.fori_loop(3 * TILES, N_A, sort, 0, unroll=2)
    r_load.wait()
    have = -1

    def begin(q):
        nonlocal have
        while have < NEED[q]:
            have += 1
            take_in(have)
        first(q)

    p_start(2)
    p_start(1)
    p_pass(2)
    p_start(3)
    p_start(0)
    pass_on(0)
    p_pass(1)
    p_done(2)
    for k in range(3):
        landed(ma.at[k], sem_ma_r.at[k])
        pltpu.make_async_copy(ma.at[k], sma.at[k + 1], sem_sma.at[k + 1]).start()
    p_pass(3)
    p_done(1)
    pltpu.make_async_copy(meta_a, sma.at[0], sem_sma.at[0]).wait()
    for k in range(3):
        pltpu.make_async_copy(ma.at[k], sma.at[k + 1], sem_sma.at[k + 1]).wait()
    p_slab(2)
    begin(0)
    pass_on(1)
    p_slab(1)
    p_done(3)
    second(0, 0)
    begin(1)
    p_slab(3)
    second(0, 1)
    p_pass(0)
    pass_on(2)
    second(1, 0)
    second(1, 1)
    p_done(0)
    begin(2)
    pass_on(3)
    p_slab(0)
    third(0)
    for q in range(3, STEPS + 2):
        if q < STEPS:
            begin(q)
        if q <= STEPS:
            second(q - 1, 0)
            second(q - 1, 1)
        if q + 1 < CHUNKS:
            pass_on(q + 1)
        third(q - 2)
        if q == STEPS - 1:
            coarse_core(0)
        if q == STEPS:
            coarse_x(0)
    coarse_core(1, order[:2])
    for k in range(4):
        coarse_x(1, order[k : k + 1])
        coarse_core(1, order[k + 2 : k + 3])
    coarse_end(0)
    coarse_end(1)

    for one in sent + ma_copies:
        one.wait_send()
    for k in (1, 2, 3):
        for one in p_copy(k):
            one.wait_send()

    @pl.when(jnp.logical_not(keeps))
    def _():
        for one in p_copy(0):
            one.wait_send()

    for one in outs:
        one.wait()


def deliver(product, coarse, product_out, coarse_out, product_here, coarse_here, sems):
    pieces = 8
    rows = product.shape[0] // pieces
    parts = [(product, product_here, product_out, pl.ds(k * rows, rows)) for k in range(pieces)]
    parts.append((coarse, coarse_here, coarse_out, pl.ds(0, coarse.shape[0])))
    loads = [pltpu.make_async_copy(a.at[p], b.at[p], sems.at[0, k]) for k, (a, b, _, p) in enumerate(parts)]
    stores = [pltpu.make_async_copy(b.at[p], c.at[p], sems.at[1, k]) for k, (_, b, c, p) in enumerate(parts)]
    for one in loads:
        one.start()
    for load, store in zip(loads, stores):
        load.wait()
        store.start()
    for one in stores:
        one.wait()


def tables(a_rows, a_cols, p_pos, aggregate, loc, meta_a, meta_p):
    shape = (128, 128)
    down = lax.broadcasted_iota(jnp.int32, shape, 0)
    along = lax.broadcasted_iota(jnp.int32, shape, 1)

    def lanes(v):
        v = jnp.concatenate([v, jnp.full((1, 128 - v.shape[1]), 1000, jnp.int32)], axis=1)
        return jnp.broadcast_to(v, shape)

    def count(hit):
        return jnp.broadcast_to(jnp.sum(jnp.where(hit, 1, 0), axis=0, keepdims=True), shape)

    def spread(index, value, fill, most):
        found = fill + jnp.sum(jnp.where(index == along, value - fill, 0), axis=0, keepdims=True)
        return jnp.clip(found, 0, most)

    here = lanes(a_rows[...])
    there = here.T
    same = (there == here) & (down < along)
    rank = count((there < here) | same).T
    slot = (here * 2 + count(same)).T
    loc[0:1] = spread(rank, down, 0, N_A - 1)
    meta_a[0:1] = spread(slot, rank, N_A, N_A)
    meta_a[1:2] = spread(slot, lanes(a_cols[...]).T, 0, 2 * N_R // RING - 1)
    meta_p[0:1] = spread(lanes(p_pos[...]).T, down, N_P, N_P)
    named = lanes(aggregate[...])
    fine = spread((named * 2 + count((named.T == named) & (down < along))).T, down, N_R, N_R)
    loc[1:2] = fine
    loc[2:3] = jnp.minimum(fine, N_R - 1)


def local(a_tiles, a_rows, a_cols, p_tiles, p_pos, r_tiles, aggregate):
    b = a_tiles.shape[-1]
    band = 2 * b
    bf, f32, i32 = jnp.bfloat16, jnp.float32, jnp.int32
    vmem, smem, dma = pltpu.VMEM, pltpu.SMEM, pltpu.SemaphoreType.DMA
    scratch = (
        [vmem((8, 128), i32), smem((8, 128), i32), vmem((8, 128), i32), vmem((8, 128), i32)]
        + [vmem((N_A, b, b), bf), vmem((N_R, b, b), bf)]
        + [vmem((N_A + 1, b, b), bf)] * 4
        + [
            vmem((3, N_A, b, b), bf),
            vmem((4, 4, N_P // RING, b, b), bf),
            vmem((4, 4, N_P // RING, b, b), bf),
            vmem((2, N_P + 1, b, b), bf),
            vmem((4, 2 * N_R, b, band), bf),
            vmem((STEPS, PARTS, b, b), bf),
            vmem((STEPS, 2, PARTS // 2, b, b), bf),
            vmem((STEPS, 2, PARTS, b, b), bf),
            vmem((STEPS, 2, PARTS, b, b), bf),
            vmem((2, N_R + 1, b, b), bf),
            vmem((2, 4, 4, b, b), bf),
            vmem((2, 4, 4, b, b), bf),
            vmem((2, 3, 4, b, b), bf),
            vmem((2, 3, 4, b, b), bf),
            vmem((3, 8, 128), i32),
            vmem((4, 8, 128), i32),
            vmem((4, 8, 128), i32),
            smem((4, 8, 128), i32),
            smem((4, 8, 128), i32),
            smem((4, 8, 128), i32),
        ]
        + [dma((4, CHUNKS)), dma((4, CHUNKS))]
        + [dma((4,))] * 2
        + [dma((4, 4))] * 4
        + [dma((3,))] * 2
        + [dma((4,))] * 4
        + [dma((STEPS, 2))] * 4
        + [dma((2, 4))] * 2
        + [dma((2, 3))] * 2
        + [dma((4,)), dma((4,)), dma((4,)), dma((STEPS, 2)), dma((2,)), dma]
    )
    in_vmem = pl.BlockSpec(memory_space=pltpu.VMEM)
    anywhere = pl.BlockSpec(memory_space=pl.ANY)
    product, coarse = pl.pallas_call(
        kernel,
        out_shape=(
            jax.ShapeDtypeStruct((N_R, b, band), bf),
            jax.ShapeDtypeStruct((4, b, band), f32),
        ),
        in_specs=[in_vmem] * 4 + [anywhere] * 3,
        out_specs=(anywhere, in_vmem),
        scratch_shapes=scratch,
        compiler_params=pltpu.CompilerParams(
            collective_id=0, has_side_effects=True, vmem_limit_bytes=60 * 1024 * 1024
        ),
        cost_estimate=pl.CostEstimate(flops=9 * 10**9, bytes_accessed=10**7, transcendentals=0),
    )(a_rows, a_cols, p_pos.T, aggregate.T, a_tiles[0], p_tiles[:, 0], r_tiles)
    product, coarse = pl.pallas_call(
        deliver,
        out_shape=(jax.ShapeDtypeStruct(product.shape, bf), jax.ShapeDtypeStruct(coarse.shape, f32)),
        in_specs=[anywhere, anywhere],
        out_specs=(anywhere, anywhere),
        scratch_shapes=[vmem(product.shape, bf), vmem(coarse.shape, f32), dma((2, 9))],
    )(product, coarse)
    return product.reshape(N_R * b, band), coarse.reshape(4 * b, band)


def solution(mesh):
    in_specs = (
        P("row", "col", None, None),
        P("row", "col"),
        P("row", "col"),
        P("row", "col", None, None),
        P("row", "col"),
        P("row", None, None),
        P("row", None),
    )
    out_specs = (P("row", "col"), P("row", "col"))
    return jax.shard_map(local, mesh=mesh, in_specs=in_specs, out_specs=out_specs, check_vma=False)
```
